256 devices in a mesh: seq: 32 (over y, z), mp: 8 (over x, core).
Axes of the slice: x: 4, y: 4, z: 8, core: 2. Of those that a mesh axis runs over, the one named last changes fastest.
Arguments:
- patch_hidden: bfloat16 [16384, 5120], P('seq', 'mp'), may hold values from -6 to 6
- out_weight: bfloat16 [5120, 8192], P(None, 'mp'), may hold values from -0.078125 to 0.078125
- out_bias: bfloat16 [8192], P('mp'), may hold values from -3 to 3
- cluster_ids: int32 [16384], P('seq'), may hold values from 0 to 8191, as said below
- memory_slots: bfloat16 [8192, 8192], P('seq', 'mp'), may hold values from -6 to 6
- slot_counts: int32 [8192], P('seq'), may hold values from 1 to 16
- norm_gain: bfloat16 [8192], P('mp'), may hold values from 0.099609375 to 1.8984375
- key_weight: bfloat16 [8192, 1024], P('seq', 'mp'), may hold values from -0.0625 to 0.0625
- value_weight: bfloat16 [8192, 1024], P('seq', 'mp'), may hold values from -0.0625 to 0.0625
- key_bias: bfloat16 [1024], P('mp'), may hold values from -3 to 3
- value_bias: bfloat16 [1024], P('mp'), may hold values from -3 to 3
Outputs:
- memory_new: bfloat16 [8192, 8192], P('seq', 'mp')
- slot_keys: bfloat16 [8192, 1024], P('seq', 'mp')
- slot_values: bfloat16 [8192, 1024], P('seq', 'mp')
The draws below stay inside these ranges and needn't reach their ends.
Inputs may be any that keep to these rules, and one draw needn't show every extreme that they name: `cluster_ids`: slots s * 256 to (s + 1) * 256 - 1 belong to index s of seq. Of the 512 rows of one index of seq, at most 48 name slots of any one index of seq, and in every draw some index of seq receives exactly 48 rows from every index of seq.
All inputs are finite; a program needn't handle non-finite values.
Results may differ from the reference program's by a relative error of at most 0.0054.
Values may be sent and summed in bfloat16 or wider, within the bound.
A program may use at most 128 MiB of HBM per device.

```python
import jax
import jax.numpy as jnp
from jax import lax

D = 8192
HIDDEN_M = 5120
ROWS_DEV = 512
SLOT_DEV = 256
KVW = 1024
ROWS = 16384
SLOTS = 8192
HOT = 4
CAP = 48
N_SEQ = 32


def draw_cluster_ids(key, part):
    owner_key, order_key, local_key = jax.random.split(jax.random.fold_in(key, 17), 3)
    owner_of_rank = jax.random.permutation(owner_key, N_SEQ)
    rank_index = jnp.arange(N_SEQ, dtype=jnp.int32)
    remaining = ROWS_DEV - HOT * CAP
    base_count = remaining // (N_SEQ - HOT)
    extra_count = remaining % (N_SEQ - HOT)
    per_rank = jnp.where(rank_index < HOT, CAP, base_count + (rank_index - HOT < extra_count).astype(jnp.int32))
    rank_ends = jnp.cumsum(per_rank).astype(jnp.int32)
    position = jnp.arange(ROWS_DEV, dtype=jnp.int32)
    rank_of_position = jnp.sum((position[:, None] >= rank_ends[None, :]).astype(jnp.int32), axis=1)
    sorted_owner = owner_of_rank[rank_of_position]
    block_keys = jax.random.split(order_key, N_SEQ)

    def shuffle_block(block_key):
        return sorted_owner[jax.random.permutation(block_key, ROWS_DEV)]
    owners = jax.vmap(shuffle_block)(block_keys).reshape(ROWS)
    local_slot = jax.random.randint(local_key, (ROWS,), 0, SLOT_DEV)
    return (owners * SLOT_DEV + local_slot).astype(jnp.int32)


def touch_ends(result, own_key, low, high):
    longest = result.shape.index(max(result.shape))
    spots = []
    for shift in (0, 1):
        where = [jax.random.randint(jax.random.fold_in(own_key, axis), (), 0, length) for axis, length in enumerate(result.shape)]
        where[longest] = (where[longest] + shift) % result.shape[longest]
        spots.append(tuple(where))
    return result.at[spots[0]].set(low).at[spots[1]].set(high)


def levels(stream_key, extent, cuts, low, top_value):
    loudness, own = 1.0, jax.random.fold_in(stream_key, 6)
    for dim, shards_of in cuts:
        draws = jnp.exp(jax.random.uniform(jax.random.fold_in(own, dim), (shards_of,), jnp.float32, low / len(cuts), top_value / len(cuts)))
        loudness = loudness * jnp.repeat(draws, extent[dim] // shards_of).reshape([-1 if axis == dim else 1 for axis in range(len(extent))])
    return loudness


def normal_values(key, extent, scale, limit, cuts=(), held_as=jnp.bfloat16):
    entries = jax.random.normal(key, extent, jnp.float32) * scale
    if len(cuts) > 0:
        entries = levels(key, extent, cuts, -0.22, 0.18) * entries
    return jnp.clip(entries, min=-limit, max=limit).astype(held_as)


def setup_inputs(seed: int = 0) -> dict:
    seeds = jax.random.split(jax.random.key(seed), 12)
    return {
        "patch_hidden": normal_values(seeds[0], (ROWS, HIDDEN_M), 1.0, 6.0, ((0, 32), (1, 8))),
        "out_weight": normal_values(seeds[1], (HIDDEN_M, D), HIDDEN_M ** -0.5, 0.078125, ((1, 8),)),
        "out_bias": normal_values(seeds[2], (D,), 0.5, 3.0, ((0, 8),)),
        "cluster_ids": draw_cluster_ids(jax.random.fold_in(seeds[11], 71), 0),
        "memory_slots": normal_values(seeds[4], (SLOTS, D), 1.0, 6.0, ((0, 32), (1, 8))),
        "slot_counts": touch_ends(jax.random.randint(seeds[5], (SLOTS,), 1, 17), jax.random.fold_in(seeds[5], 1), 1, 16).astype(jnp.int32),
        "norm_gain": jnp.clip(1.0 + 0.18 * jax.random.normal(seeds[6], (D,), jnp.float32), 0.099609375, 1.8984375).astype(jnp.bfloat16),
        "key_weight": normal_values(seeds[7], (D, KVW), D ** -0.5, 0.0625, ((0, 32), (1, 8))),
        "value_weight": normal_values(seeds[8], (D, KVW), D ** -0.5, 0.0625, ((0, 32), (1, 8))),
        "key_bias": normal_values(seeds[9], (KVW,), 0.5, 3.0, ((0, 8),)),
        "value_bias": normal_values(seeds[10], (KVW,), 0.5, 3.0, ((0, 8),)),
    }


def reference(patch_hidden, out_weight, out_bias, cluster_ids, memory_slots, slot_counts, norm_gain, key_weight, value_weight, key_bias, value_bias):
    blocked = patch_hidden.reshape(N_SEQ, ROWS_DEV, HIDDEN_M)
    id_blocks = cluster_ids.reshape(N_SEQ, ROWS_DEV)

    def fold_block(carry, inputs):
        totals, arrivals = carry
        block_rows, block_ids = inputs
        hidden = jax.nn.gelu(block_rows.astype(jnp.float32), approximate=False).astype(jnp.bfloat16)
        merged = jnp.dot(hidden, out_weight, preferred_element_type=jnp.float32) + out_bias.astype(jnp.float32)
        totals = totals + jax.ops.segment_sum(merged, block_ids, num_segments=SLOTS)
        arrivals = arrivals + jax.ops.segment_sum(jnp.ones((ROWS_DEV,), jnp.float32), block_ids, num_segments=SLOTS)
        return ((totals, arrivals), block_ids)
    start_state = (jnp.zeros((SLOTS, D), jnp.float32), jnp.zeros((SLOTS,), jnp.float32))
    final_state, unused_ids = lax.scan(fold_block, start_state, (blocked, id_blocks))
    totals, arrivals = final_state
    weight = slot_counts.astype(jnp.float32)
    memory_new = ((weight[:, None] * memory_slots.astype(jnp.float32) + totals) / (weight + arrivals)[:, None]).astype(jnp.bfloat16)
    stored = lax.optimization_barrier(memory_new).astype(jnp.float32)
    inverse = lax.rsqrt(lax.optimization_barrier(jnp.sum(stored * stored, axis=1)) / D + 1e-06)
    normed = (stored * inverse[:, None] * norm_gain.astype(jnp.float32)[None, :]).astype(jnp.bfloat16)
    slot_keys = (jnp.dot(normed, key_weight, preferred_element_type=jnp.float32) + key_bias.astype(jnp.float32)).astype(jnp.bfloat16)
    slot_values = (jnp.dot(normed, value_weight, preferred_element_type=jnp.float32) + value_bias.astype(jnp.float32)).astype(jnp.bfloat16)
    return (memory_new, slot_keys, slot_values)
```

```python
import jax
import jax.numpy as jnp
from jax import lax
from jax.experimental import pallas as pl
from jax.experimental.pallas import tpu as pltpu
from jax.sharding import PartitionSpec as P

D = 8192
CHUNKS = ((0, 256), (256, 256), (512, 128))
MESH = pl.DeviceIdType.MESH
N_REMOTE = 110
N_LOCAL = 12
F32, BF16 = jnp.float32, jnp.bfloat16


def gelu(v):
    return v * (1.0 + lax.erf(v * 0.7071067811865476)) * 0.5


def kernel(
    patch,
    wout,
    bias,
    ids,
    mem,
    counts,
    gain,
    kw,
    vw,
    kb,
    vb,
    mem_out,
    key_out,
    val_out,
    pv0,
    pv1,
    pv2,
    h0,
    h1,
    h2,
    idsb,
    oh,
    sp0,
    sp1,
    sp2,
    sm0,
    sm1,
    sm2,
    rp0,
    rp1,
    rp2,
    rm0,
    rm1,
    rm2,
    hs0,
    hs1,
    hs2,
    wv,
    mv,
    acc,
    kvown,
    wkv,
    gbuf,
    mnew,
    ks,
    kr,
    k1s,
    k1r,
    k2s,
    k2r,
    sq,
    kout,
    vout,
    ssem,
    rsem,
    lsem,
):
    pv, h = (pv0, pv1, pv2), (h0, h1, h2)
    sp, sm, rp, rm = (sp0, sp1, sp2), (sm0, sm1, sm2), (rp0, rp1, rp2), (rm0, rm1, rm2)
    hs = (hs0, hs1, hs2)
    seq, mp = lax.axis_index("seq"), lax.axis_index("mp")
    y, z = lax.div(seq, 8), lax.rem(seq, 8)
    x, c = lax.div(mp, 2), lax.rem(mp, 2)

    def m4(v):
        return lax.rem(v + 4, 4)

    def m8(v):
        return lax.rem(v + 8, 8)

    def dev(dy=0, dz=0, dx=0, other=False):
        return (m4(y + dy) * 8 + m8(z + dz), m4(x + dx) * 2 + (1 - c if other else c))

    yp, ym = dev(dy=1), dev(dy=-1)
    zp, zm = dev(dz=1), dev(dz=-1)
    xp, xm = dev(dx=1), dev(dx=-1)
    sib = dev(other=True)
    perm_to = (x * 8 + lax.rem(2 * lax.rem(z, 4) + c + 4, 8), lax.div(seq, 4))
    q = lax.rem(z + 4, 8)
    perm_from = (x * 8 + 4 * c + lax.div(q, 2), 2 * y + lax.rem(q, 2))

    used = [0, 0]
    sends = []

    def remote(src, dst, to, land=None):
        i = used[0]
        used[0] += 1
        copy = pltpu.make_async_remote_copy(
            src_ref=src,
            dst_ref=dst,
            send_sem=ssem.at[i],
            recv_sem=rsem.at[i],
            device_id=to,
            device_id_type=MESH,
        )
        copy.start()
        sends.append(copy)
        if land is None:
            return copy
        return pltpu.make_async_remote_copy(
            src_ref=land,
            dst_ref=land,
            send_sem=ssem.at[i],
            recv_sem=rsem.at[i],
            device_id=to,
            device_id_type=MESH,
        )

    def local(src, dst):
        i = used[1]
        used[1] += 1
        copy = pltpu.make_async_copy(src, dst, lsem.at[i])
        copy.start()
        return copy

    barrier = pltpu.get_barrier_semaphore()
    partners = [yp, ym, zp, zm, perm_to, perm_from, sib]
    partners += [dev(dx=d, other=o) for d in (1, 2, 3) for o in (False, True)]
    for partner in partners:
        pl.semaphore_signal(barrier, inc=1, device_id=partner, device_id_type=MESH)

    got_patch = [local(patch.at[:, pl.ds(o, w)], pv[i]) for i, (o, w) in enumerate(CHUNKS)]
    got_kw = local(kw, kvown.at[:, pl.ds(0, 128)])
    got_vw = local(vw, kvown.at[:, pl.ds(128, 128)])
    got_mem = local(mem, mv)
    got_w = local(wout, wv)

    idsb[0, 0] = ids[...]

    def activate(i):
        got_patch[i].wait()

        def body(r, carry):
            part = pl.ds(pl.multiple_of(r * 64, 64), 64)
            h[i][0, part, :] = gelu(pv[i][part, :].astype(F32)).astype(BF16)
            return carry

        lax.fori_loop(0, 8, body, 0)

    activate(0)
    got_kw.wait()
    got_vw.wait()
    pl.semaphore_wait(barrier, len(partners))

    yc = [{} for _ in CHUNKS]

    def y_first(i):
        yc[i]["p"] = remote(h[i].at[0], h[i].at[1], yp)
        yc[i]["m"] = remote(h[i].at[0], h[i].at[2], ym)

    def y_fwd(i):
        yc[i]["p"].wait_recv()
        yc[i]["fp"] = remote(h[i].at[1, pl.ds(0, 256)], h[i].at[3, pl.ds(0, 256)], yp)
        yc[i]["m"].wait_recv()
        yc[i]["fm"] = remote(h[i].at[2, pl.ds(256, 256)], h[i].at[3, pl.ds(256, 256)], ym)

    def y_done(i):
        yc[i]["fp"].wait_recv()
        yc[i]["fm"].wait_recv()

    wc = {}

    def w_perm():
        wc["perm"] = remote(kvown, wkv.at[perm_to_y, perm_to_z], perm_to, land=wkv.at[y, z])

    perm_to_y = x
    perm_to_z = lax.rem(2 * lax.rem(z, 4) + c + 4, 8)

    def w_z(t):
        if t == 1:
            wc["perm"].wait_recv()
        else:
            wc["zp", t - 1].wait_recv()
            wc["zm", t - 1].wait_recv()
        if t <= 3:
            a, b = m8(z - t + 1), m8(z + t - 1)
            wc["zp", t] = remote(wkv.at[y, a], wkv.at[y, a], zp, land=wkv.at[y, m8(z - t)])
            wc["zm", t] = remote(wkv.at[y, b], wkv.at[y, b], zm, land=wkv.at[y, m8(z + t)])
        else:
            a, b, f = m8(z - 3), m8(z + 3), m8(z + 4)
            lo, hi = pl.ds(0, 128), pl.ds(128, 128)
            wc["zp", 4] = remote(wkv.at[y, a, lo], wkv.at[y, a, lo], zp, land=wkv.at[y, f, lo])
            wc["zm", 4] = remote(wkv.at[y, b, hi], wkv.at[y, b, hi], zm, land=wkv.at[y, f, hi])

    def w_y(t):
        if t == 1:
            wc["zp", 4].wait_recv()
            wc["zm", 4].wait_recv()
            wc["yp"] = remote(wkv.at[y], wkv.at[y], yp, land=wkv.at[m4(y - 1)])
            wc["ym"] = remote(wkv.at[y], wkv.at[y], ym, land=wkv.at[m4(y + 1)])
        else:
            a, b, f = m4(y - 1), m4(y + 1), m4(y + 2)
            lo, hi = pl.ds(0, 4), pl.ds(4, 4)
            wc["yp"].wait_recv()
            wc["fp"] = remote(wkv.at[a, lo], wkv.at[a, lo], yp, land=wkv.at[f, lo])
            wc["ym"].wait_recv()
            wc["fm"] = remote(wkv.at[b, hi], wkv.at[b, hi], ym, land=wkv.at[f, hi])

    def w_done():
        wc["fp"].wait_recv()
        wc["fm"].wait_recv()

    ic = {}

    def i_first():
        ic["p"] = remote(idsb.at[0, 0], idsb.at[0, 1], yp)
        ic["m"] = remote(idsb.at[0, 0], idsb.at[0, 2], ym)

    def i_fwd():
        ic["p"].wait_recv()
        ic["f"] = remote(idsb.at[0, 1], idsb.at[0, 3], yp)

    def i_z(t):
        if t == 1:
            ic["m"].wait_recv()
            ic["f"].wait_recv()
            ic["zp", 1] = remote(idsb.at[0], idsb.at[1], zp)
            ic["zm", 1] = remote(idsb.at[0], idsb.at[5], zm)
        else:
            ic["zp", t - 1].wait_recv()
            ic["zp", t] = remote(idsb.at[t - 1], idsb.at[t], zp)
            if t <= 3:
                ic["zm", t - 1].wait_recv()
                ic["zm", t] = remote(idsb.at[3 + t], idsb.at[4 + t], zm)

    def i_done():
        ic["zp", 4].wait_recv()
        ic["zm", 3].wait_recv()

    def onehot(lo, hi):
        def body(k, carry):
            step = lax.div(k + 1, 2)
            zrel = 4 + step * (1 - 2 * lax.rem(k, 2))
            base = (y * 8 + m8(z + zrel)) * 256
            slot = lax.broadcasted_iota(jnp.int32, (256, 128), 0)
            for s in range(4):
                block = idsb[0, s]
                for r in range(4):
                    row = block[r : r + 1, :] - base
                    hit = jnp.where(slot == row, 1.0, 0.0).astype(BF16)
                    oh[k, :, s * 512 + r * 128 : s * 512 + (r + 1) * 128] = hit
            return carry

        lax.fori_loop(lo, hi, body, 0)

    def sums(i, k, n):
        w = CHUNKS[i][1]
        left = oh[k : k + n].reshape(n * 256, 2048)
        return jnp.dot(left, h[i][...].reshape(2048, w), preferred_element_type=F32)

    rc = [{} for _ in CHUNKS]
    lo, hi = pl.ds(0, 128), pl.ds(128, 128)

    def rs(i, t):
        if t == 0:
            p = sums(i, 0, 1).astype(BF16)
            sp[i][0, lo] = p[:128]
            sm[i][0, hi] = p[128:]
            rc[i]["p", 0] = remote(sp[i].at[0, lo], rp[i].at[0, lo], zp)
            rc[i]["m", 0] = remote(sm[i].at[0, hi], rm[i].at[0, hi], zm)
            return
        p = sums(i, 2 * t - 1, 2)
        rc[i]["p", t - 1].wait_recv()
        if t == 1:
            sp[i][t, lo] = (p[:128] + rp[i][0, lo].astype(F32)).astype(BF16)
            sp[i][t, hi] = p[128:256].astype(BF16)
        else:
            sp[i][t] = (p[:256] + rp[i][t - 1].astype(F32)).astype(BF16)
        rc[i]["p", t] = remote(sp[i].at[t], rp[i].at[t], zp)
        rc[i]["m", t - 1].wait_recv()
        if t == 1:
            sm[i][t, lo] = p[256:384].astype(BF16)
            sm[i][t, hi] = (p[384:] + rm[i][0, hi].astype(F32)).astype(BF16)
        else:
            sm[i][t] = (p[256:] + rm[i][t - 1].astype(F32)).astype(BF16)
        rc[i]["m", t] = remote(sm[i].at[t], rm[i].at[t], zm)

    xc = [{} for _ in CHUNKS]

    def rs_end(i):
        p = sums(i, 7, 1)
        rc[i]["p", 3].wait_recv()
        rc[i]["m", 3].wait_recv()
        hs[i][0] = (p + rp[i][3].astype(F32) + rm[i][3].astype(F32)).astype(BF16)
        xc[i][2] = remote(hs[i].at[0], hs[i].at[2], xp)
        xc[i][4] = remote(hs[i].at[0], hs[i].at[4], xm)
        xc[i][1] = remote(hs[i].at[0], hs[i].at[1], sib)

    def x_fwd(i):
        xc[i][2].wait_recv()
        xc[i]["fp"] = remote(hs[i].at[2, lo], hs[i].at[6, lo], xp)
        xc[i][3] = remote(hs[i].at[2], hs[i].at[3], sib)
        xc[i][4].wait_recv()
        xc[i]["fm"] = remote(hs[i].at[4, hi], hs[i].at[6, hi], xm)
        xc[i][5] = remote(hs[i].at[4], hs[i].at[5], sib)

    def x_last(i):
        xc[i]["fp"].wait_recv()
        xc[i]["fm"].wait_recv()
        xc[i][7] = remote(hs[i].at[6], hs[i].at[7], sib)

    def mm(i, blocks, first=False):
        off, w = CHUNKS[i]
        for b in blocks:
            if b % 2:
                xc[i][b].wait_recv()
            xs = m4(x + (0, -1, 1, 2)[b // 2])
            src = xs * 2 + (1 - c if b % 2 else c)
            got = jnp.dot(hs[i][b], wv[src, off : off + w, :], preferred_element_type=F32)
            acc[...] = got if first and b == blocks[0] else acc[...] + got

    y_first(0)
    w_perm()
    i_first()
    activate(1)
    i_fwd()
    activate(2)
    w_z(1)
    i_z(1)
    onehot(0, 3)
    y_fwd(0)
    y_first(1)
    w_z(2)
    i_z(2)
    onehot(3, 8)
    w_z(3)
    i_z(3)
    y_done(0)
    rs(0, 0)
    w_z(4)
    i_z(4)
    rs(0, 1)
    y_fwd(1)
    y_first(2)
    rs(0, 2)
    y_done(1)
    rs(1, 0)
    rs(0, 3)
    rs(1, 1)
    y_fwd(2)
    w_y(1)
    rs_end(0)
    rs(1, 2)
    y_done(2)
    rs(2, 0)
    x_fwd(0)
    rs(1, 3)
    got_w.wait()
    mm(0, (0, 1), first=True)
    rs(2, 1)
    x_last(0)
    rs_end(1)
    rs(2, 2)
    mm(0, (2, 3, 4, 5))
    rs(2, 3)
    x_fwd(1)

    i_done()
    own = seq * 256

    def count(p, carry):
        slot = lax.broadcasted_iota(jnp.int32, (256, 128), 0) + own
        for s in range(4):
            block = idsb[p, s]
            for r in range(4):
                carry = carry + jnp.where(slot == block[r : r + 1, :], 1.0, 0.0)
        return carry

    hits = lax.fori_loop(0, 8, count, jnp.zeros((256, 128), F32))
    arrivals = jnp.broadcast_to(jnp.sum(hits, axis=1, keepdims=True), (256, 128))
    weight = jnp.transpose(jnp.broadcast_to(counts[...].astype(F32), (128, 256)))
    share = 1.0 / (weight + arrivals)

    mm(0, (6, 7))
    rs_end(2)
    x_last(1)
    mm(1, (0, 1, 2, 3, 4, 5))
    x_fwd(2)
    mm(2, (0, 1))
    mm(1, (6, 7))
    x_last(2)
    mm(2, (2, 3, 4, 5))
    w_y(2)
    mm(2, (6, 7))

    got_mem.wait()
    squares = jnp.zeros((256, 128), F32)
    for j in range(8):
        col = slice(j * 128, (j + 1) * 128)
        b = bias[:, col].astype(F32)
        total = acc[:, col] + arrivals * b
        new = ((weight * mv[:, col].astype(F32) + total) * share).astype(BF16)
        mnew[:, col] = new
        stored = new.astype(F32)
        squares = squares + stored * stored
        gbuf[:, col] = (stored * gain[:, col].astype(F32)).astype(BF16)
    put_mem = local(mnew, mem_out)
    mine = jnp.broadcast_to(jnp.sum(squares, axis=1, keepdims=True), (256, 128))
    sq[0] = jnp.transpose(mine)[:8, :]
    sqc = []
    for d in (0, 1, 2, 3):
        for o in (False, True):
            if d or o:
                slot = 2 * d + o
                sqc.append(remote(sq.at[0], sq.at[slot], dev(dx=d, other=o)))

    w_done()

    def heads(d, o):
        ys = m4(x + d)
        core = 1 - c if o else c
        total = None
        for r in range(4):
            zs = lax.rem(2 * r + core + 4, 8)
            part = jnp.dot(
                gbuf[:, r * 256 : (r + 1) * 256], wkv[ys, zs], preferred_element_type=F32
            )
            total = part if total is None else total + part
        return total

    kc = {}
    for d in (2, 1, 3, 0):
        ks[d] = heads(d, True).astype(BF16)
        kc[d] = remote(ks.at[d], kr.at[d], sib)
    p = heads(2, False)
    kc[2].wait_recv()
    p = (p + kr[2].astype(F32)).astype(BF16)
    k1s[...] = p
    kc["p1"] = remote(k1s.at[lo], k1r.at[lo], xp)
    kc["m1"] = remote(k1s.at[hi], k1r.at[hi], xm)
    for d, half, key, to in ((1, 0, "p", xp), (3, 1, "m", xm)):
        p = heads(d, False)
        kc[d].wait_recv()
        p = p + kr[d].astype(F32)
        kc[key + "1"].wait_recv()
        if half == 0:
            k2s[half, lo] = (p[:128] + k1r[lo].astype(F32)).astype(BF16)
            k2s[half, hi] = p[128:].astype(BF16)
        else:
            k2s[half, lo] = p[:128].astype(BF16)
            k2s[half, hi] = (p[128:] + k1r[hi].astype(F32)).astype(BF16)
        kc[key + "2"] = remote(k2s.at[half], k2r.at[half], to)
    p = heads(0, False)
    kc[0].wait_recv()
    p = p + kr[0].astype(F32)
    for copy in sqc:
        copy.wait_recv()
    whole = sq[0]
    for j in range(1, 8):
        whole = whole + sq[j]
    inverse = lax.rsqrt(whole[:1, :] * (1.0 / D) + 1e-06)
    inverse = jnp.transpose(jnp.broadcast_to(inverse, (128, 256)))
    kc["p2"].wait_recv()
    kc["m2"].wait_recv()
    p = p + k2r[0].astype(F32) + k2r[1].astype(F32)
    kout[...] = (p[:, :128] * inverse + kb[...].astype(F32)).astype(BF16)
    vout[...] = (p[:, 128:] * inverse + vb[...].astype(F32)).astype(BF16)
    put_key = local(kout, key_out)
    put_val = local(vout, val_out)
    for copy in sends:
        copy.wait_send()
    put_mem.wait()
    put_key.wait()
    put_val.wait()


def on_device(patch, wout, bias, ids, mem, counts, gain, kw, vw, kb, vb):
    any_, vmem = pl.BlockSpec(memory_space=pl.ANY), pl.BlockSpec(memory_space=pltpu.VMEM)

    def per_chunk(*shape):
        return [pltpu.VMEM((*shape, w), BF16) for _, w in CHUNKS]

    scratch = [
        *per_chunk(512),
        *per_chunk(4, 512),
        pltpu.VMEM((8, 4, 4, 128), jnp.int32),
        pltpu.VMEM((8, 256, 2048), BF16),
        *per_chunk(4, 256),
        *per_chunk(4, 256),
        *per_chunk(4, 256),
        *per_chunk(4, 256),
        *per_chunk(8, 256),
        pltpu.VMEM((8, 640, 1024), BF16),
        pltpu.VMEM((256, 1024), BF16),
        pltpu.VMEM((256, 1024), F32),
        pltpu.VMEM((256, 256), BF16),
        pltpu.VMEM((4, 8, 256, 256), BF16),
        pltpu.VMEM((256, 1024), BF16),
        pltpu.VMEM((256, 1024), BF16),
        pltpu.VMEM((4, 256, 256), BF16),
        pltpu.VMEM((4, 256, 256), BF16),
        pltpu.VMEM((256, 256), BF16),
        pltpu.VMEM((256, 256), BF16),
        pltpu.VMEM((2, 256, 256), BF16),
        pltpu.VMEM((2, 256, 256), BF16),
        pltpu.VMEM((8, 8, 256), F32),
        pltpu.VMEM((256, 128), BF16),
        pltpu.VMEM((256, 128), BF16),
        pltpu.SemaphoreType.DMA((N_REMOTE,)),
        pltpu.SemaphoreType.DMA((N_REMOTE,)),
        pltpu.SemaphoreType.DMA((N_LOCAL,)),
    ]
    return pl.pallas_call(
        kernel,
        out_shape=(
            jax.ShapeDtypeStruct((256, 1024), BF16),
            jax.ShapeDtypeStruct((256, 128), BF16),
            jax.ShapeDtypeStruct((256, 128), BF16),
        ),
        in_specs=[any_, any_, vmem, vmem, any_, vmem, vmem, any_, any_, vmem, vmem],
        out_specs=(any_, any_, any_),
        scratch_shapes=scratch,
        compiler_params=pltpu.CompilerParams(
            collective_id=0, has_side_effects=True, vmem_limit_bytes=58 * 2**20
        ),
        cost_estimate=pl.CostEstimate(
            flops=10_000_000_000, bytes_accessed=20_000_000, transcendentals=330_000
        ),
    )(
        patch,
        wout.reshape(8, 640, 1024),
        bias.reshape(1, 1024),
        ids.reshape(4, 128),
        mem,
        counts.reshape(1, 256),
        gain.reshape(1, 1024),
        kw,
        vw,
        kb.reshape(1, 128),
        vb.reshape(1, 128),
    )


def solution(mesh):
    return jax.shard_map(
        on_device,
        mesh=mesh,
        in_specs=(
            P("seq", "mp"),
            P(None, "mp"),
            P("mp"),
            P("seq"),
            P("seq", "mp"),
            P("seq"),
            P("mp"),
            P("seq", "mp"),
            P("seq", "mp"),
            P("mp"),
            P("mp"),
        ),
        out_specs=(P("seq", "mp"), P("seq", "mp"), P("seq", "mp")),
        check_vma=False,
    )
```

```python
import jax
import jax.numpy as jnp
from jax import lax
from jax.experimental import pallas as pl
from jax.experimental.pallas import tpu as pltpu
from jax.sharding import PartitionSpec as P

D = 8192
CHUNKS = ((0, 256), (256, 256), (512, 128))
MESH = pl.DeviceIdType.MESH
N_REMOTE = 110
N_LOCAL = 12
F32, BF16 = jnp.float32, jnp.bfloat16


def gelu(v):
    return v * (1.0 + lax.erf(v * 0.7071067811865476)) * 0.5


def kernel(
    patch,
    wout,
    bias,
    ids,
    mem,
    counts,
    gain,
    kw,
    vw,
    kb,
    vb,
    mem_out,
    key_out,
    val_out,
    pv0,
    pv1,
    pv2,
    h0,
    h1,
    h2,
    idsb,
    oh,
    sp0,
    sp1,
    sp2,
    sm0,
    sm1,
    sm2,
    rp0,
    rp1,
    rp2,
    rm0,
    rm1,
    rm2,
    hs0,
    hs1,
    hs2,
    wv,
    mv,
    acc,
    kvown,
    wkv,
    gbuf,
    mnew,
    ks,
    kr,
    k1s,
    k1r,
    k2s,
    k2r,
    sq,
    kout,
    vout,
    ssem,
    rsem,
    lsem,
):
    pv, h = (pv0, pv1, pv2), (h0, h1, h2)
    sp, sm, rp, rm = (sp0, sp1, sp2), (sm0, sm1, sm2), (rp0, rp1, rp2), (rm0, rm1, rm2)
    hs = (hs0, hs1, hs2)
    seq, mp = lax.axis_index("seq"), lax.axis_index("mp")
    y, z = lax.div(seq, 8), lax.rem(seq, 8)
    x, c = lax.div(mp, 2), lax.rem(mp, 2)

    def m4(v):
        return lax.rem(v + 4, 4)

    def m8(v):
        return lax.rem(v + 8, 8)

    def dev(dy=0, dz=0, dx=0, other=False):
        return (m4(y + dy) * 8 + m8(z + dz), m4(x + dx) * 2 + (1 - c if other else c))

    yp, ym = dev(dy=1), dev(dy=-1)
    zp, zm = dev(dz=1), dev(dz=-1)
    xp, xm = dev(dx=1), dev(dx=-1)
    sib = dev(other=True)
    perm_to = (x * 8 + lax.rem(2 * lax.rem(z, 4) + c + 4, 8), lax.div(seq, 4))
    q = lax.rem(z + 4, 8)
    perm_from = (x * 8 + 4 * c + lax.div(q, 2), 2 * y + lax.rem(q, 2))

    used = [0, 0]
    sends = []

    def remote(src, dst, to, land=None):
        i = used[0]
        used[0] += 1
        copy = pltpu.make_async_remote_copy(
            src_ref=src,
            dst_ref=dst,
            send_sem=ssem.at[i],
            recv_sem=rsem.at[i],
            device_id=to,
            device_id_type=MESH,
        )
        copy.start()
        sends.append(copy)
        if land is None:
            return copy
        return pltpu.make_async_remote_copy(
            src_ref=land,
            dst_ref=land,
            send_sem=ssem.at[i],
            recv_sem=rsem.at[i],
            device_id=to,
            device_id_type=MESH,
        )

    def local(src, dst):
        i = used[1]
        used[1] += 1
        copy = pltpu.make_async_copy(src, dst, lsem.at[i])
        copy.start()
        return copy

    barrier = pltpu.get_barrier_semaphore()
    partners = [yp, ym, zp, zm, perm_to, perm_from, sib]
    partners += [dev(dx=d, other=o) for d in (1, 2, 3) for o in (False, True)]
    for partner in partners:
        pl.semaphore_signal(barrier, inc=1, device_id=partner, device_id_type=MESH)

    got_patch = [local(patch.at[:, pl.ds(o, w)], pv[i]) for i, (o, w) in enumerate(CHUNKS)]
    got_kw = local(kw, kvown.at[:, pl.ds(0, 128)])
    got_vw = local(vw, kvown.at[:, pl.ds(128, 128)])
    got_mem = local(mem, mv)
    got_w = local(wout, wv)

    idsb[0, 0] = ids[...]

    def activate(i):
        got_patch[i].wait()

        def body(r, carry):
            part = pl.ds(pl.multiple_of(r * 64, 64), 64)
            h[i][0, part, :] = gelu(pv[i][part, :].astype(F32)).astype(BF16)
            return carry

        lax.fori_loop(0, 8, body, 0)

    activate(0)
    got_kw.wait()
    got_vw.wait()
    pl.semaphore_wait(barrier, len(partners))

    yc = [{} for _ in CHUNKS]

    def y_first(i):
        yc[i]["p"] = remote(h[i].at[0], h[i].at[1], yp)
        yc[i]["m"] = remote(h[i].at[0], h[i].at[2], ym)

    def y_fwd(i):
        yc[i]["p"].wait_recv()
        yc[i]["fp"] = remote(h[i].at[1, pl.ds(0, 256)], h[i].at[3, pl.ds(0, 256)], yp)
        yc[i]["m"].wait_recv()
        yc[i]["fm"] = remote(h[i].at[2, pl.ds(256, 256)], h[i].at[3, pl.ds(256, 256)], ym)

    def y_done(i):
        yc[i]["fp"].wait_recv()
        yc[i]["fm"].wait_recv()

    wc = {}

    def w_perm():
        wc["perm"] = remote(kvown, wkv.at[perm_to_y, perm_to_z], perm_to, land=wkv.at[y, z])

    perm_to_y = x
    perm_to_z = lax.rem(2 * lax.rem(z, 4) + c + 4, 8)

    def w_z(t):
        if t == 1:
            wc["perm"].wait_recv()
        else:
            wc["zp", t - 1].wait_recv()
            wc["zm", t - 1].wait_recv()
        if t <= 3:
            a, b = m8(z - t + 1), m8(z + t - 1)
            wc["zp", t] = remote(wkv.at[y, a], wkv.at[y, a], zp, land=wkv.at[y, m8(z - t)])
            wc["zm", t] = remote(wkv.at[y, b], wkv.at[y, b], zm, land=wkv.at[y, m8(z + t)])
        else:
            a, b, f = m8(z - 3), m8(z + 3), m8(z + 4)
            lo, hi = pl.ds(0, 128), pl.ds(128, 128)
            wc["zp", 4] = remote(wkv.at[y, a, lo], wkv.at[y, a, lo], zp, land=wkv.at[y, f, lo])
            wc["zm", 4] = remote(wkv.at[y, b, hi], wkv.at[y, b, hi], zm, land=wkv.at[y, f, hi])

    def w_y(t):
        if t == 1:
            wc["zp", 4].wait_recv()
            wc["zm", 4].wait_recv()
            wc["yp"] = remote(wkv.at[y], wkv.at[y], yp, land=wkv.at[m4(y - 1)])
            wc["ym"] = remote(wkv.at[y], wkv.at[y], ym, land=wkv.at[m4(y + 1)])
        else:
            a, b, f = m4(y - 1), m4(y + 1), m4(y + 2)
            lo, hi = pl.ds(0, 4), pl.ds(4, 4)
            wc["yp"].wait_recv()
            wc["fp"] = remote(wkv.at[a, lo], wkv.at[a, lo], yp, land=wkv.at[f, lo])
            wc["ym"].wait_recv()
            wc["fm"] = remote(wkv.at[b, hi], wkv.at[b, hi], ym, land=wkv.at[f, hi])

    def w_done():
        wc["fp"].wait_recv()
        wc["fm"].wait_recv()

    ic = {}

    def i_first():
        ic["p"] = remote(idsb.at[0, 0], idsb.at[0, 1], yp)
        ic["m"] = remote(idsb.at[0, 0], idsb.at[0, 2], ym)

    def i_fwd():
        ic["p"].wait_recv()
        ic["f"] = remote(idsb.at[0, 1], idsb.at[0, 3], yp)

    def i_z(t):
        if t == 1:
            ic["m"].wait_recv()
            ic["f"].wait_recv()
            ic["zp", 1] = remote(idsb.at[0], idsb.at[1], zp)
            ic["zm", 1] = remote(idsb.at[0], idsb.at[5], zm)
        else:
            ic["zp", t - 1].wait_recv()
            ic["zp", t] = remote(idsb.at[t - 1], idsb.at[t], zp)
            if t <= 3:
                ic["zm", t - 1].wait_recv()
                ic["zm", t] = remote(idsb.at[3 + t], idsb.at[4 + t], zm)

    def i_done():
        ic["zp", 4].wait_recv()
        ic["zm", 3].wait_recv()

    def onehot(lo, hi):
        def body(k, carry):
            step = lax.div(k + 1, 2)
            zrel = 4 + step * (1 - 2 * lax.rem(k, 2))
            base = (y * 8 + m8(z + zrel)) * 256
            slot = lax.broadcasted_iota(jnp.int32, (256, 128), 0)
            for s in range(4):
                block = idsb[0, s]
                for r in range(4):
                    row = block[r : r + 1, :] - base
                    hit = jnp.where(slot == row, 1.0, 0.0).astype(BF16)
                    oh[k, :, s * 512 + r * 128 : s * 512 + (r + 1) * 128] = hit
            return carry

        lax.fori_loop(lo, hi, body, 0)

    def sums(i, k, n):
        w = CHUNKS[i][1]
        left = oh[k : k + n].reshape(n * 256, 2048)
        return jnp.dot(left, h[i][...].reshape(2048, w), preferred_element_type=F32)

    rc = [{} for _ in CHUNKS]
    lo, hi = pl.ds(0, 128), pl.ds(128, 128)

    def rs(i, t):
        if t == 0:
            p = sums(i, 0, 1).astype(BF16)
            sp[i][0, lo] = p[:128]
            sm[i][0, hi] = p[128:]
            rc[i]["p", 0] = remote(sp[i].at[0, lo], rp[i].at[0, lo], zp)
            rc[i]["m", 0] = remote(sm[i].at[0, hi], rm[i].at[0, hi], zm)
            return
        p = sums(i, 2 * t - 1, 2)
        rc[i]["p", t - 1].wait_recv()
        if t == 1:
            sp[i][t, lo] = (p[:128] + rp[i][0, lo].astype(F32)).astype(BF16)
            sp[i][t, hi] = p[128:256].astype(BF16)
        else:
            sp[i][t] = (p[:256] + rp[i][t - 1].astype(F32)).astype(BF16)
        rc[i]["p", t] = remote(sp[i].at[t], rp[i].at[t], zp)
        rc[i]["m", t - 1].wait_recv()
        if t == 1:
            sm[i][t, lo] = p[256:384].astype(BF16)
            sm[i][t, hi] = (p[384:] + rm[i][0, hi].astype(F32)).astype(BF16)
        else:
            sm[i][t] = (p[256:] + rm[i][t - 1].astype(F32)).astype(BF16)
        rc[i]["m", t] = remote(sm[i].at[t], rm[i].at[t], zm)

    xc = [{} for _ in CHUNKS]

    def rs_end(i):
        p = sums(i, 7, 1)
        rc[i]["p", 3].wait_recv()
        rc[i]["m", 3].wait_recv()
        hs[i][0] = (p + rp[i][3].astype(F32) + rm[i][3].astype(F32)).astype(BF16)
        xc[i][2] = remote(hs[i].at[0], hs[i].at[2], xp)
        xc[i][4] = remote(hs[i].at[0], hs[i].at[4], xm)
        xc[i][1] = remote(hs[i].at[0], hs[i].at[1], sib)

    def x_fwd(i):
        xc[i][2].wait_recv()
        xc[i]["fp"] = remote(hs[i].at[2, lo], hs[i].at[6, lo], xp)
        xc[i][3] = remote(hs[i].at[2], hs[i].at[3], sib)
        xc[i][4].wait_recv()
        xc[i]["fm"] = remote(hs[i].at[4, hi], hs[i].at[6, hi], xm)
        xc[i][5] = remote(hs[i].at[4], hs[i].at[5], sib)

    def x_last(i):
        xc[i]["fp"].wait_recv()
        xc[i]["fm"].wait_recv()
        xc[i][7] = remote(hs[i].at[6], hs[i].at[7], sib)

    def mm(i, blocks, first=False):
        off, w = CHUNKS[i]
        for b in blocks:
            if b % 2:
                xc[i][b].wait_recv()
            xs = m4(x + (0, -1, 1, 2)[b // 2])
            src = xs * 2 + (1 - c if b % 2 else c)
            got = jnp.dot(hs[i][b], wv[src, off : off + w, :], preferred_element_type=F32)
            acc[...] = got if first and b == blocks[0] else acc[...] + got

    w_perm()
    y_first(0)
    activate(1)
    w_z(1)
    i_first()
    y_first(1)
    i_fwd()
    w_z(2)
    activate(2)
    y_fwd(0)
    y_first(2)
    w_z(3)
    i_z(1)
    onehot(0, 1)
    onehot(1, 8)
    y_fwd(1)
    w_z(4)
    y_done(0)
    rs(0, 0)
    y_fwd(2)
    w_y(1)
    y_done(1)
    rs(1, 0)
    rs(0, 1)
    rs(1, 1)
    rs(0, 2)
    y_done(2)
    rs(2, 0)
    rs(1, 2)
    rs(2, 1)
    rs(0, 3)
    i_z(2)
    rs(2, 2)
    rs(1, 3)
    rs_end(0)
    got_w.wait()
    mm(0, (0, 1), first=True)
    i_z(3)
    rs(2, 3)
    w_y(2)
    rs_end(1)
    i_z(4)
    rs_end(2)
    i_done()
    own = seq * 256

    def count(p, carry):
        slot = lax.broadcasted_iota(jnp.int32, (256, 128), 0) + own
        for s in range(4):
            block = idsb[p, s]
            for r in range(4):
                carry = carry + jnp.where(slot == block[r : r + 1, :], 1.0, 0.0)
        return carry

    hits = lax.fori_loop(0, 8, count, jnp.zeros((256, 128), F32))
    arrivals = jnp.broadcast_to(jnp.sum(hits, axis=1, keepdims=True), (256, 128))
    weight = jnp.transpose(jnp.broadcast_to(counts[...].astype(F32), (128, 256)))
    share = 1.0 / (weight + arrivals)
    x_fwd(0)
    x_fwd(1)
    mm(1, (2, 3))
    x_fwd(2)
    mm(2, (0, 1))
    mm(2, (2, 3))
    mm(0, (2, 3))
    mm(1, (4, 5))
    mm(2, (4, 5))
    mm(0, (4, 5))
    x_last(0)
    mm(1, (0, 1))
    x_last(1)
    x_last(2)
    mm(0, (6, 7))
    mm(1, (6, 7))
    mm(2, (6, 7))

    got_mem.wait()
    squares = jnp.zeros((256, 128), F32)
    for j in range(8):
        col = slice(j * 128, (j + 1) * 128)
        b = bias[j : j + 1, :].astype(F32)
        total = acc[:, col] + arrivals * b
        new = ((weight * mv[:, col].astype(F32) + total) * share).astype(BF16)
        mnew[:, col] = new
        stored = new.astype(F32)
        squares = squares + stored * stored
        gbuf[:, col] = (stored * gain[j : j + 1, :].astype(F32)).astype(BF16)
    put_mem = local(mnew, mem_out)
    mine = jnp.broadcast_to(jnp.sum(squares, axis=1, keepdims=True), (256, 128))
    sq[0] = jnp.transpose(mine)[:8, :]
    sqc = []
    for d in (0, 1, 2, 3):
        for o in (False, True):
            if d or o:
                slot = 2 * d + o
                sqc.append(remote(sq.at[0], sq.at[slot], dev(dx=d, other=o)))

    w_done()

    def heads(d, o):
        ys = m4(x + d)
        core = 1 - c if o else c
        total = None
        for r in range(4):
            zs = lax.rem(2 * r + core + 4, 8)
            part = jnp.dot(
                gbuf[:, r * 256 : (r + 1) * 256], wkv[ys, zs], preferred_element_type=F32
            )
            total = part if total is None else total + part
        return total

    kc = {}
    for d in (2, 1, 3, 0):
        ks[d] = heads(d, True).astype(BF16)
        kc[d] = remote(ks.at[d], kr.at[d], sib)
    p = heads(2, False)
    kc[2].wait_recv()
    p = (p + kr[2].astype(F32)).astype(BF16)
    k1s[...] = p
    kc["p1"] = remote(k1s.at[lo], k1r.at[lo], xp)
    kc["m1"] = remote(k1s.at[hi], k1r.at[hi], xm)
    for d, half, key, to in ((1, 0, "p", xp), (3, 1, "m", xm)):
        p = heads(d, False)
        kc[d].wait_recv()
        p = p + kr[d].astype(F32)
        kc[key + "1"].wait_recv()
        if half == 0:
            k2s[half, lo] = (p[:128] + k1r[lo].astype(F32)).astype(BF16)
            k2s[half, hi] = p[128:].astype(BF16)
        else:
            k2s[half, lo] = p[:128].astype(BF16)
            k2s[half, hi] = (p[128:] + k1r[hi].astype(F32)).astype(BF16)
        kc[key + "2"] = remote(k2s.at[half], k2r.at[half], to)
    p = heads(0, False)
    kc[0].wait_recv()
    p = p + kr[0].astype(F32)
    for copy in sqc:
        copy.wait_recv()
    whole = sq[0]
    for j in range(1, 8):
        whole = whole + sq[j]
    inverse = lax.rsqrt(whole[:1, :] * (1.0 / D) + 1e-06)
    inverse = jnp.transpose(jnp.broadcast_to(inverse, (128, 256)))
    kc["p2"].wait_recv()
    kc["m2"].wait_recv()
    p = p + k2r[0].astype(F32) + k2r[1].astype(F32)
    kout[...] = (p[:, :128] * inverse + kb[...].astype(F32)).astype(BF16)
    vout[...] = (p[:, 128:] * inverse + vb[...].astype(F32)).astype(BF16)
    put_key = local(kout, key_out)
    put_val = local(vout, val_out)
    for copy in sends:
        copy.wait_send()
    put_mem.wait()
    put_key.wait()
    put_val.wait()


def hand_over(a, b, c, x, y, z, sem):
    copies = [
        pltpu.make_async_copy(s, d, sem.at[i]) for i, (s, d) in enumerate(((a, x), (b, y), (c, z)))
    ]
    for copy in copies:
        copy.start()
    for copy in copies:
        copy.wait()


def on_device(patch, wout, bias, ids, mem, counts, gain, kw, vw, kb, vb):
    any_, vmem = pl.BlockSpec(memory_space=pl.ANY), pl.BlockSpec(memory_space=pltpu.VMEM)

    def per_chunk(*shape):
        return [pltpu.VMEM((*shape, w), BF16) for _, w in CHUNKS]

    scratch = [
        *per_chunk(512),
        *per_chunk(4, 512),
        pltpu.VMEM((8, 4, 4, 128), jnp.int32),
        pltpu.VMEM((8, 256, 2048), BF16),
        *per_chunk(4, 256),
        *per_chunk(4, 256),
        *per_chunk(4, 256),
        *per_chunk(4, 256),
        *per_chunk(8, 256),
        pltpu.VMEM((8, 640, 1024), BF16),
        pltpu.VMEM((256, 1024), BF16),
        pltpu.VMEM((256, 1024), F32),
        pltpu.VMEM((256, 256), BF16),
        pltpu.VMEM((4, 8, 256, 256), BF16),
        pltpu.VMEM((256, 1024), BF16),
        pltpu.VMEM((256, 1024), BF16),
        pltpu.VMEM((4, 256, 256), BF16),
        pltpu.VMEM((4, 256, 256), BF16),
        pltpu.VMEM((256, 256), BF16),
        pltpu.VMEM((256, 256), BF16),
        pltpu.VMEM((2, 256, 256), BF16),
        pltpu.VMEM((2, 256, 256), BF16),
        pltpu.VMEM((8, 8, 256), F32),
        pltpu.VMEM((256, 128), BF16),
        pltpu.VMEM((256, 128), BF16),
        pltpu.SemaphoreType.DMA((N_REMOTE,)),
        pltpu.SemaphoreType.DMA((N_REMOTE,)),
        pltpu.SemaphoreType.DMA((N_LOCAL,)),
    ]
    made = pl.pallas_call(
        kernel,
        out_shape=(
            jax.ShapeDtypeStruct((256, 1024), BF16),
            jax.ShapeDtypeStruct((256, 128), BF16),
            jax.ShapeDtypeStruct((256, 128), BF16),
        ),
        in_specs=[any_, any_, vmem, vmem, any_, vmem, vmem, any_, any_, vmem, vmem],
        out_specs=(any_, any_, any_),
        scratch_shapes=scratch,
        compiler_params=pltpu.CompilerParams(
            collective_id=0, has_side_effects=True, vmem_limit_bytes=58 * 2**20
        ),
        cost_estimate=pl.CostEstimate(
            flops=10_000_000_000, bytes_accessed=20_000_000, transcendentals=330_000
        ),
    )(
        patch,
        wout.reshape(8, 640, 1024),
        bias.reshape(8, 128),
        ids.reshape(4, 128),
        mem,
        counts.reshape(1, 256),
        gain.reshape(8, 128),
        kw,
        vw,
        kb.reshape(1, 128),
        vb.reshape(1, 128),
    )
    return pl.pallas_call(
        hand_over,
        out_shape=tuple(jax.ShapeDtypeStruct(m.shape, m.dtype) for m in made),
        in_specs=[any_, any_, any_],
        out_specs=(vmem, vmem, vmem),
        scratch_shapes=[pltpu.SemaphoreType.DMA((3,))],
    )(*made)


def solution(mesh):
    return jax.shard_map(
        on_device,
        mesh=mesh,
        in_specs=(
            P("seq", "mp"),
            P(None, "mp"),
            P("mp"),
            P("seq"),
            P("seq", "mp"),
            P("seq"),
            P("mp"),
            P("seq", "mp"),
            P("seq", "mp"),
            P("mp"),
            P("mp"),
        ),
        out_specs=(P("seq", "mp"), P("seq", "mp"), P("seq", "mp")),
        check_vma=False,
    )
```

```python
import jax
import jax.numpy as jnp
from jax import lax
from jax.experimental import pallas as pl
from jax.experimental.pallas import tpu as pltpu
from jax.sharding import PartitionSpec as P

D = 8192
CHUNKS = ((0, 256), (256, 256), (512, 128))
GROUPS = ((0,), (1,), (2,))
ROWS_B = 32
MESH = pl.DeviceIdType.MESH
N_REMOTE = 160
N_LOCAL = 12
F32, BF16 = jnp.float32, jnp.bfloat16

ORDER = (
    ("w_perm",),
    ("i_first",),
    ("y_first", 0),
    ("i_fwd",),
    ("act", 1),
    ("w_z", 1, 0),
    ("y_first", 1),
    ("w_z", 1, 1),
    ("oh", 0),
    ("y_fwd", 0, 1),
    ("i_z", 1),
    ("w_z", 2, 1),
    ("y_fwd", 0, 0),
    ("w_z", 2, 0),
    ("oh", 1),
    ("act", 2),
    ("i_z", 2),
    ("w_z", 3, 0),
    ("y_fwd", 1, 1),
    ("y_fwd", 1, 0),
    ("w_z", 3, 1),
    ("y_first", 2),
    ("rs", 0, 0),
    ("w_z", 4, 0),
    ("i_z", 3),
    ("w_z", 4, 1),
    ("b_y", 1, 1),
    ("rs", 1, 0),
    ("b_y", 1, 0),
    ("rs", 0, 1),
    ("y_fwd", 2, 1),
    ("y_fwd", 2, 0),
    ("i_z", 4),
    ("b_y", 2, 0),
    ("w_y", 1, 0),
    ("b_y", 2, 1),
    ("w_y", 1, 1),
    ("rs", 1, 1),
    ("rs", 2, 0),
    ("rs", 0, 2),
    ("rs", 2, 1),
    ("rs", 1, 2),
    ("rs", 0, 3),
    ("rs", 2, 2),
    ("rs", 1, 3),
    ("b_z", 1, 1),
    ("count",),
    ("b_z", 1, 0),
    ("rs_end", 0),
    ("rs", 2, 3),
    ("rs_end", 1),
    ("b_z", 2, 1),
    ("w_y", 2, 1),
    ("w_y", 2, 0),
    ("b_z", 2, 0),
    ("rs_end", 2),
    ("x_fwd", 0, 0),
    ("x_fwd", 0, 1),
    ("x_fwd", 1, 1),
    ("x_fwd", 1, 0),
    ("mm", 0, 1),
    ("mm", 0, 0),
    ("b_z", 3, 0),
    ("mm", 0, 2),
    ("b_z", 3, 1),
    ("x_fwd", 2, 1),
    ("mm", 1, 2),
    ("mm", 1, 1),
    ("mm", 2, 0),
    ("x_fwd", 2, 0),
    ("mm", 2, 2),
    ("mm", 1, 0),
    ("x_last", 0),
    ("b_z", 4, 0),
    ("x_last", 1),
    ("mm", 0, 3),
    ("b_z", 4, 1),
    ("mm", 1, 3),
    ("x_last", 2),
    ("mm", 2, 1),
    ("mm", 2, 3),
)


def gelu(v):
    return v * (1.0 + lax.erf(v * 0.7071067811865476)) * 0.5


def kernel(*refs):
    n = len(CHUNKS)
    it = iter(refs)

    def take(k):
        return [next(it) for _ in range(k)]

    patch, wout, bias, ids, mem, counts, gain, kw, vw, kb, vb = take(11)
    mem_out, key_out, val_out = take(3)
    pv, h = take(n), take(n)
    idsb, oh = take(2)
    sp, sm, rp, rm, hs = (take(n) for _ in range(5))
    wv, mv, acc, kvown, wkv, gbuf, mnew, ks, kr = take(9)
    k1s, k1r, k2s, k2r, sq, kout, vout, ssem, rsem, lsem = take(10)
    seq, mp = lax.axis_index("seq"), lax.axis_index("mp")
    y, z = lax.div(seq, 8), lax.rem(seq, 8)
    x, c = lax.div(mp, 2), lax.rem(mp, 2)

    def m4(v):
        return lax.rem(v + 4, 4)

    def m8(v):
        return lax.rem(v + 8, 8)

    def dev(dy=0, dz=0, dx=0, other=False):
        return (m4(y + dy) * 8 + m8(z + dz), m4(x + dx) * 2 + (1 - c if other else c))

    yp, ym = dev(dy=1), dev(dy=-1)
    zp, zm = dev(dz=1), dev(dz=-1)
    xp, xm = dev(dx=1), dev(dx=-1)
    sib = dev(other=True)
    perm_to = (x * 8 + lax.rem(2 * lax.rem(z, 4) + c + 4, 8), lax.div(seq, 4))
    q = lax.rem(z + 4, 8)
    perm_from = (x * 8 + 4 * c + lax.div(q, 2), 2 * y + lax.rem(q, 2))

    used = [0, 0]
    sends = []

    def remote(src, dst, to, land=None):
        i = used[0]
        used[0] += 1
        copy = pltpu.make_async_remote_copy(
            src_ref=src,
            dst_ref=dst,
            send_sem=ssem.at[i],
            recv_sem=rsem.at[i],
            device_id=to,
            device_id_type=MESH,
        )
        copy.start()
        sends.append(copy)
        if land is None:
            return copy
        return pltpu.make_async_remote_copy(
            src_ref=land,
            dst_ref=land,
            send_sem=ssem.at[i],
            recv_sem=rsem.at[i],
            device_id=to,
            device_id_type=MESH,
        )

    def local(src, dst):
        i = used[1]
        used[1] += 1
        copy = pltpu.make_async_copy(src, dst, lsem.at[i])
        copy.start()
        return copy

    barrier = pltpu.get_barrier_semaphore()
    partners = [yp, ym, zp, zm, perm_to, perm_from, sib]
    partners += [dev(dx=d, other=o) for d in (1, 2, 3) for o in (False, True)]
    for partner in partners:
        pl.semaphore_signal(barrier, inc=1, device_id=partner, device_id_type=MESH)

    got_patch = [local(patch.at[:, pl.ds(o, w)], pv[i]) for i, (o, w) in enumerate(CHUNKS)]
    got_kw = local(kw, kvown.at[:, pl.ds(0, 128)])
    got_vw = local(vw, kvown.at[:, pl.ds(128, 128)])
    got_mem = local(mem, mv)
    got_w = local(wout, wv)

    idsb[0, 0] = ids[...]

    def activate(i):
        got_patch[i].wait()

        def body(r, carry):
            part = pl.ds(pl.multiple_of(r * 64, 64), 64)
            h[i][0, part, :] = gelu(pv[i][part, :].astype(F32)).astype(BF16)
            return carry

        lax.fori_loop(0, 8, body, 0)

    got_kw.wait()
    got_vw.wait()
    activate(0)
    pl.semaphore_wait(barrier, len(partners))

    yc = [{} for _ in CHUNKS]

    def y_first(i):
        yc[i]["p"] = remote(h[i].at[0], h[i].at[1], yp)
        yc[i]["m"] = remote(h[i].at[0], h[i].at[2], ym)

    def y_fwd(i, back):
        if not back:
            yc[i]["p"].wait_recv()
            part = pl.ds(0, 256)
            yc[i]["fp"] = remote(h[i].at[1, part], h[i].at[3, part], yp)
        else:
            yc[i]["m"].wait_recv()
            part = pl.ds(256, 256)
            yc[i]["fm"] = remote(h[i].at[2, part], h[i].at[3, part], ym)

    wc = {}
    rows_a, rows_b = pl.ds(0, 256 - ROWS_B), pl.ds(256 - ROWS_B, ROWS_B)
    half_a = [pl.ds(0, 128 - ROWS_B // 2), pl.ds(128 - ROWS_B // 2, 128 - ROWS_B // 2)]
    half_b = [pl.ds(256 - ROWS_B, ROWS_B // 2), pl.ds(256 - ROWS_B // 2, ROWS_B // 2)]
    perm_to_z = lax.rem(2 * lax.rem(z, 4) + c + 4, 8)

    def same(where, land, to):
        return remote(wkv.at[where], wkv.at[where], to, land=wkv.at[land])

    def once(key):
        copy = wc.pop(key, None)
        if copy is not None:
            copy.wait_recv()

    def w_perm():
        wc["perm"] = remote(kvown, wkv.at[x, perm_to_z], perm_to, land=wkv.at[y, z])

    def w_z(t, back):
        once("perm")
        once(("z", t - 1, back))
        sign, to = (-1, zm) if back else (1, zp)
        src, land = m8(z - sign * (t - 1)), m8(z - sign * t)
        part = rows_a if t <= 3 else half_a[back]
        wc["z", t, back] = same((y, src, part), (y, land, part), to)

    def w_y(t, back):
        sign, to = (-1, ym) if back else (1, yp)
        if t == 1:
            once(("z", 4, 0))
            once(("z", 4, 1))
            every = pl.ds(0, 8)
            wc["y", 1, back] = same((y, every, rows_a), (m4(y - sign), every, rows_a), to)
        else:
            once(("y", 1, back))
            some = pl.ds(4 * back, 4)
            wc["y", 2, back] = same(
                (m4(y - sign), some, rows_a), (m4(y - 2 * sign), some, rows_a), to
            )

    def b_y(t, back):
        sign, to = (-1, ym) if back else (1, yp)
        once("perm")
        once(("b", t - 1, back))
        part = rows_b if t == 1 else half_b[back]
        src, land = m4(y - sign * (t - 1)), m4(y - sign * t)
        wc["b", t, back] = same((src, z, part), (land, z, part), to)

    def b_z(t, back):
        sign, to = (-1, zm) if back else (1, zp)
        if t == 1:
            once(("b", 2, 0))
            once(("b", 2, 1))
        once(("c", t - 1, back))
        some = pl.ds(0, 4) if t <= 3 else pl.ds(2 * back, 2)
        src, land = m8(z - sign * (t - 1)), m8(z - sign * t)
        wc["c", t, back] = same((some, src, rows_b), (some, land, rows_b), to)

    ic = {}

    def i_first():
        ic["p"] = remote(idsb.at[0, 0], idsb.at[0, 1], yp)
        ic["m"] = remote(idsb.at[0, 0], idsb.at[0, 2], ym)

    def i_fwd():
        ic["p"].wait_recv()
        ic["f"] = remote(idsb.at[0, 1], idsb.at[0, 3], yp)

    def i_plane():
        for key in ("m", "f"):
            copy = ic.pop(key, None)
            if copy is not None:
                copy.wait_recv()

    def i_z(t):
        if t == 1:
            i_plane()
            ic["zp", 1] = remote(idsb.at[0], idsb.at[1], zp)
            ic["zm", 1] = remote(idsb.at[0], idsb.at[5], zm)
        else:
            ic["zp", t - 1].wait_recv()
            ic["zp", t] = remote(idsb.at[t - 1], idsb.at[t], zp)
            if t <= 3:
                ic["zm", t - 1].wait_recv()
                ic["zm", t] = remote(idsb.at[3 + t], idsb.at[4 + t], zm)

    def onehot(second):
        i_plane()

        def body(k, carry):
            step = lax.div(k + 1, 2)
            zrel = 4 + step * (1 - 2 * lax.rem(k, 2))
            base = (y * 8 + m8(z + zrel)) * 256
            slot = lax.broadcasted_iota(jnp.int32, (256, 128), 0)
            for s in range(4):
                block = idsb[0, s]
                for r in range(4):
                    row = block[r : r + 1, :] - base
                    hit = jnp.where(slot == row, 1.0, 0.0).astype(BF16)
                    oh[k, :, s * 512 + r * 128 : s * 512 + (r + 1) * 128] = hit
            return carry

        lax.fori_loop(1 if second else 0, 8 if second else 1, body, 0)

    def sums(i, k, m):
        w = CHUNKS[i][1]
        left = oh[k : k + m].reshape(m * 256, 2048)
        return jnp.dot(left, h[i][...].reshape(2048, w), preferred_element_type=F32)

    rc = [{} for _ in CHUNKS]
    lo, hi = pl.ds(0, 128), pl.ds(128, 128)

    def rs(i, t):
        if t == 0:
            yc[i]["fp"].wait_recv()
            yc[i]["fm"].wait_recv()
            p = sums(i, 0, 1).astype(BF16)
            sp[i][0, lo] = p[:128]
            sm[i][0, hi] = p[128:]
            rc[i]["p", 0] = remote(sp[i].at[0, lo], rp[i].at[0, lo], zp)
            rc[i]["m", 0] = remote(sm[i].at[0, hi], rm[i].at[0, hi], zm)
            return
        p = sums(i, 2 * t - 1, 2)
        rc[i]["p", t - 1].wait_recv()
        if t == 1:
            sp[i][t, lo] = (p[:128] + rp[i][0, lo].astype(F32)).astype(BF16)
            sp[i][t, hi] = p[128:256].astype(BF16)
        else:
            sp[i][t] = (p[:256] + rp[i][t - 1].astype(F32)).astype(BF16)
        rc[i]["p", t] = remote(sp[i].at[t], rp[i].at[t], zp)
        rc[i]["m", t - 1].wait_recv()
        if t == 1:
            sm[i][t, lo] = p[256:384].astype(BF16)
            sm[i][t, hi] = (p[384:] + rm[i][0, hi].astype(F32)).astype(BF16)
        else:
            sm[i][t] = (p[256:] + rm[i][t - 1].astype(F32)).astype(BF16)
        rc[i]["m", t] = remote(sm[i].at[t], rm[i].at[t], zm)

    xc = [{} for _ in CHUNKS]

    def rs_end(i):
        p = sums(i, 7, 1)
        rc[i]["p", 3].wait_recv()
        rc[i]["m", 3].wait_recv()
        hs[i][0] = (p + rp[i][3].astype(F32) + rm[i][3].astype(F32)).astype(BF16)
        xc[i][2] = remote(hs[i].at[0], hs[i].at[2], xp)
        xc[i][4] = remote(hs[i].at[0], hs[i].at[4], xm)
        xc[i][1] = remote(hs[i].at[0], hs[i].at[1], sib)

    def x_fwd(i, back):
        if not back:
            xc[i][2].wait_recv()
            xc[i]["fp"] = remote(hs[i].at[2, lo], hs[i].at[6, lo], xp)
            xc[i][3] = remote(hs[i].at[2], hs[i].at[3], sib)
        else:
            xc[i][4].wait_recv()
            xc[i]["fm"] = remote(hs[i].at[4, hi], hs[i].at[6, hi], xm)
            xc[i][5] = remote(hs[i].at[4], hs[i].at[5], sib)

    def x_last(i):
        xc[i]["fp"].wait_recv()
        xc[i]["fm"].wait_recv()
        xc[i][7] = remote(hs[i].at[6], hs[i].at[7], sib)

    def mm(group, pair):
        chunks = GROUPS[group]
        for i in chunks:
            xc[i][2 * pair + 1].wait_recv()
        off, w = CHUNKS[chunks[0]][0], sum(CHUNKS[i][1] for i in chunks)
        if not state.get("acc"):
            got_w.wait()
        got = None
        for b in (2 * pair, 2 * pair + 1):
            src = m4(x + (0, -1, 1, 2)[pair]) * 2 + (1 - c if b % 2 else c)
            left = jnp.concatenate([hs[i][b] for i in chunks], axis=1)
            part = jnp.dot(left, wv[src, off : off + w, :], preferred_element_type=F32)
            got = part if got is None else got + part
        if state.get("acc"):
            acc[...] = acc[...] + got
        else:
            acc[...] = got
            state["acc"] = True

    state = {}

    def count():
        ic["zp", 4].wait_recv()
        ic["zm", 3].wait_recv()
        own = seq * 256

        def body(p, carry):
            slot = lax.broadcasted_iota(jnp.int32, (256, 128), 0) + own
            for s in range(4):
                block = idsb[p, s]
                for r in range(4):
                    carry = carry + jnp.where(slot == block[r : r + 1, :], 1.0, 0.0)
            return carry

        hits = lax.fori_loop(0, 8, body, jnp.zeros((256, 128), F32))
        state["arrivals"] = jnp.broadcast_to(jnp.sum(hits, axis=1, keepdims=True), (256, 128))
        weight = jnp.transpose(jnp.broadcast_to(counts[...].astype(F32), (128, 256)))
        state["weight"] = weight
        state["share"] = 1.0 / (weight + state["arrivals"])

    table = {
        "act": activate,
        "y_first": y_first,
        "y_fwd": y_fwd,
        "w_perm": w_perm,
        "w_z": w_z,
        "w_y": w_y,
        "b_y": b_y,
        "b_z": b_z,
        "i_first": i_first,
        "i_fwd": i_fwd,
        "i_z": i_z,
        "oh": onehot,
        "rs": rs,
        "rs_end": rs_end,
        "x_fwd": x_fwd,
        "x_last": x_last,
        "mm": mm,
        "count": count,
    }
    for event, *where in ORDER:
        table[event](*where)
    arrivals, weight, share = state["arrivals"], state["weight"], state["share"]

    got_mem.wait()
    squares = jnp.zeros((256, 128), F32)
    for j in range(8):
        col = slice(j * 128, (j + 1) * 128)
        b = bias[j : j + 1, :].astype(F32)
        total = acc[:, col] + arrivals * b
        new = ((weight * mv[:, col].astype(F32) + total) * share).astype(BF16)
        mnew[:, col] = new
        stored = new.astype(F32)
        squares = squares + stored * stored
        gbuf[:, col] = (stored * gain[j : j + 1, :].astype(F32)).astype(BF16)
    put_mem = local(mnew, mem_out)
    mine = jnp.broadcast_to(jnp.sum(squares, axis=1, keepdims=True), (256, 128))
    sq[0] = jnp.transpose(mine)[:8, :]
    sqc = []
    for d in (0, 1, 2, 3):
        for o in (False, True):
            if d or o:
                slot = 2 * d + o
                sqc.append(remote(sq.at[0], sq.at[slot], dev(dx=d, other=o)))

    for key in list(wc):
        once(key)

    def heads(d, o):
        ys = m4(x + d)
        core = 1 - c if o else c
        total = None
        for r in range(4):
            zs = lax.rem(2 * r + core + 4, 8)
            part = jnp.dot(
                gbuf[:, r * 256 : (r + 1) * 256], wkv[ys, zs], preferred_element_type=F32
            )
            total = part if total is None else total + part
        return total

    kc = {}
    for d in (2, 1, 3, 0):
        ks[d] = heads(d, True).astype(BF16)
        kc[d] = remote(ks.at[d], kr.at[d], sib)
    p = heads(2, False)
    kc[2].wait_recv()
    p = (p + kr[2].astype(F32)).astype(BF16)
    k1s[...] = p
    kc["p1"] = remote(k1s.at[lo], k1r.at[lo], xp)
    kc["m1"] = remote(k1s.at[hi], k1r.at[hi], xm)
    for d, half, key, to in ((1, 0, "p", xp), (3, 1, "m", xm)):
        p = heads(d, False)
        kc[d].wait_recv()
        p = p + kr[d].astype(F32)
        kc[key + "1"].wait_recv()
        if half == 0:
            k2s[half, lo] = (p[:128] + k1r[lo].astype(F32)).astype(BF16)
            k2s[half, hi] = p[128:].astype(BF16)
        else:
            k2s[half, lo] = p[:128].astype(BF16)
            k2s[half, hi] = (p[128:] + k1r[hi].astype(F32)).astype(BF16)
        kc[key + "2"] = remote(k2s.at[half], k2r.at[half], to)
    p = heads(0, False)
    kc[0].wait_recv()
    p = p + kr[0].astype(F32)
    for copy in sqc:
        copy.wait_recv()
    whole = sq[0]
    for j in range(1, 8):
        whole = whole + sq[j]
    inverse = lax.rsqrt(whole[:1, :] * (1.0 / D) + 1e-06)
    inverse = jnp.transpose(jnp.broadcast_to(inverse, (128, 256)))
    kc["p2"].wait_recv()
    kc["m2"].wait_recv()
    p = p + k2r[0].astype(F32) + k2r[1].astype(F32)
    kout[...] = (p[:, :128] * inverse + kb[...].astype(F32)).astype(BF16)
    vout[...] = (p[:, 128:] * inverse + vb[...].astype(F32)).astype(BF16)
    put_key = local(kout, key_out)
    put_val = local(vout, val_out)
    for copy in sends:
        copy.wait_send()
    put_mem.wait()
    put_key.wait()
    put_val.wait()


def hand_over(a, b, c, x, y, z, sem):
    copies = [
        pltpu.make_async_copy(s, d, sem.at[i]) for i, (s, d) in enumerate(((a, x), (b, y), (c, z)))
    ]
    for copy in copies:
        copy.start()
    for copy in copies:
        copy.wait()


def on_device(patch, wout, bias, ids, mem, counts, gain, kw, vw, kb, vb):
    any_, vmem = pl.BlockSpec(memory_space=pl.ANY), pl.BlockSpec(memory_space=pltpu.VMEM)

    def per_chunk(*shape):
        return [pltpu.VMEM((*shape, w), BF16) for _, w in CHUNKS]

    scratch = [
        *per_chunk(512),
        *per_chunk(4, 512),
        pltpu.VMEM((8, 4, 4, 128), jnp.int32),
        pltpu.VMEM((8, 256, 2048), BF16),
        *per_chunk(4, 256),
        *per_chunk(4, 256),
        *per_chunk(4, 256),
        *per_chunk(4, 256),
        *per_chunk(8, 256),
        pltpu.VMEM((8, 640, 1024), BF16),
        pltpu.VMEM((256, 1024), BF16),
        pltpu.VMEM((256, 1024), F32),
        pltpu.VMEM((256, 256), BF16),
        pltpu.VMEM((4, 8, 256, 256), BF16),
        pltpu.VMEM((256, 1024), BF16),
        pltpu.VMEM((256, 1024), BF16),
        pltpu.VMEM((4, 256, 256), BF16),
        pltpu.VMEM((4, 256, 256), BF16),
        pltpu.VMEM((256, 256), BF16),
        pltpu.VMEM((256, 256), BF16),
        pltpu.VMEM((2, 256, 256), BF16),
        pltpu.VMEM((2, 256, 256), BF16),
        pltpu.VMEM((8, 8, 256), F32),
        pltpu.VMEM((256, 128), BF16),
        pltpu.VMEM((256, 128), BF16),
        pltpu.SemaphoreType.DMA((N_REMOTE,)),
        pltpu.SemaphoreType.DMA((N_REMOTE,)),
        pltpu.SemaphoreType.DMA((N_LOCAL,)),
    ]
    made = pl.pallas_call(
        kernel,
        out_shape=(
            jax.ShapeDtypeStruct((256, 1024), BF16),
            jax.ShapeDtypeStruct((256, 128), BF16),
            jax.ShapeDtypeStruct((256, 128), BF16),
        ),
        in_specs=[any_, any_, vmem, vmem, any_, vmem, vmem, any_, any_, vmem, vmem],
        out_specs=(any_, any_, any_),
        scratch_shapes=scratch,
        compiler_params=pltpu.CompilerParams(
            collective_id=0, has_side_effects=True, vmem_limit_bytes=58 * 2**20
        ),
        cost_estimate=pl.CostEstimate(
            flops=10_000_000_000, bytes_accessed=20_000_000, transcendentals=330_000
        ),
    )(
        patch,
        wout.reshape(8, 640, 1024),
        bias.reshape(8, 128),
        ids.reshape(4, 128),
        mem,
        counts.reshape(1, 256),
        gain.reshape(8, 128),
        kw,
        vw,
        kb.reshape(1, 128),
        vb.reshape(1, 128),
    )
    return pl.pallas_call(
        hand_over,
        out_shape=tuple(jax.ShapeDtypeStruct(m.shape, m.dtype) for m in made),
        in_specs=[any_, any_, any_],
        out_specs=(vmem, vmem, vmem),
        scratch_shapes=[pltpu.SemaphoreType.DMA((3,))],
    )(*made)


def solution(mesh):
    return jax.shard_map(
        on_device,
        mesh=mesh,
        in_specs=(
            P("seq", "mp"),
            P(None, "mp"),
            P("mp"),
            P("seq"),
            P("seq", "mp"),
            P("seq"),
            P("mp"),
            P("seq", "mp"),
            P("seq", "mp"),
            P("mp"),
            P("mp"),
        ),
        out_specs=(P("seq", "mp"), P("seq", "mp"), P("seq", "mp")),
        check_vma=False,
    )
```

```python
import jax
import jax.numpy as jnp
from jax import lax
from jax.experimental import pallas as pl
from jax.experimental.pallas import tpu as pltpu
from jax.sharding import PartitionSpec as P

D = 8192
CHUNKS = ((0, 128), (128, 128), (256, 128), (384, 128), (512, 128))
GROUPS = ((0, 1), (2, 3), (4,))
ROWS_B = 32
MESH = pl.DeviceIdType.MESH
N_REMOTE = 160
N_LOCAL = 12
F32, BF16 = jnp.float32, jnp.bfloat16

ORDER = (
    ("w_perm",),
    ("y_first", 0),
    ("act", 2),
    ("i_first",),
    ("act", 1),
    ("y_first", 1),
    ("w_z", 1, 0),
    ("w_z", 1, 1),
    ("i_fwd",),
    ("y_first", 2),
    ("act", 4),
    ("w_z", 2, 0),
    ("y_fwd", 1, 1),
    ("y_fwd", 1, 0),
    ("w_z", 2, 1),
    ("y_fwd", 0, 0),
    ("oh", 0),
    ("act", 3),
    ("y_fwd", 0, 1),
    ("y_first", 3),
    ("oh", 1),
    ("rs", 1, 0),
    ("b_y", 1, 1),
    ("w_z", 3, 0),
    ("w_z", 3, 1),
    ("rs", 0, 0),
    ("y_first", 4),
    ("rs", 1, 1),
    ("b_y", 1, 0),
    ("y_fwd", 3, 0),
    ("b_y", 2, 1),
    ("y_fwd", 2, 0),
    ("i_z", 1),
    ("y_fwd", 3, 1),
    ("w_z", 4, 0),
    ("w_z", 4, 1),
    ("y_fwd", 2, 1),
    ("rs", 0, 1),
    ("y_fwd", 4, 0),
    ("y_fwd", 4, 1),
    ("rs", 1, 2),
    ("b_y", 2, 0),
    ("i_z", 2),
    ("rs", 3, 0),
    ("w_y", 1, 0),
    ("w_y", 1, 1),
    ("rs", 2, 0),
    ("rs", 0, 2),
    ("rs", 4, 0),
    ("rs", 1, 3),
    ("rs", 3, 1),
    ("i_z", 3),
    ("rs", 4, 1),
    ("rs", 0, 3),
    ("rs_end", 1),
    ("rs", 2, 1),
    ("rs", 4, 2),
    ("rs", 3, 2),
    ("x_fwd", 1, 0),
    ("i_z", 4),
    ("rs_end", 0),
    ("rs", 2, 2),
    ("rs", 4, 3),
    ("b_z", 1, 1),
    ("b_z", 1, 0),
    ("rs", 3, 3),
    ("rs", 2, 3),
    ("rs_end", 4),
    ("mm", 0, 0),
    ("b_z", 2, 0),
    ("x_fwd", 0, 0),
    ("x_fwd", 0, 1),
    ("w_y", 2, 0),
    ("w_y", 2, 1),
    ("x_fwd", 1, 1),
    ("b_z", 2, 1),
    ("rs_end", 3),
    ("mm", 2, 0),
    ("rs_end", 2),
    ("x_fwd", 4, 1),
    ("x_last", 0),
    ("x_fwd", 4, 0),
    ("b_z", 3, 0),
    ("b_z", 3, 1),
    ("mm", 2, 2),
    ("x_fwd", 3, 1),
    ("x_fwd", 3, 0),
    ("count",),
    ("x_last", 1),
    ("x_fwd", 2, 0),
    ("mm", 2, 1),
    ("x_fwd", 2, 1),
    ("x_last", 4),
    ("mm", 0, 2),
    ("mm", 1, 2),
    ("mm", 2, 3),
    ("mm", 1, 1),
    ("b_z", 4, 0),
    ("b_z", 4, 1),
    ("mm", 0, 1),
    ("mm", 1, 0),
    ("x_last", 3),
    ("mm", 0, 3),
    ("x_last", 2),
    ("mm", 1, 3),
)


def gelu(v):
    return v * (1.0 + lax.erf(v * 0.7071067811865476)) * 0.5


def kernel(*refs):
    n = len(CHUNKS)
    it = iter(refs)

    def take(k):
        return [next(it) for _ in range(k)]

    patch, wout, bias, ids, mem, counts, gain, kw, vw, kb, vb = take(11)
    mem_out, key_out, val_out = take(3)
    pv, h = take(n), take(n)
    idsb, oh = take(2)
    sp, sm, rp, rm, hs = (take(n) for _ in range(5))
    wv, mv, acc, kvown, wkv, gbuf, mnew, ks, kr = take(9)
    k1s, k1r, k2s, k2r, sq, kout, vout, ssem, rsem, lsem = take(10)
    seq, mp = lax.axis_index("seq"), lax.axis_index("mp")
    y, z = lax.div(seq, 8), lax.rem(seq, 8)
    x, c = lax.div(mp, 2), lax.rem(mp, 2)

    def m4(v):
        return lax.rem(v + 4, 4)

    def m8(v):
        return lax.rem(v + 8, 8)

    def dev(dy=0, dz=0, dx=0, other=False):
        return (m4(y + dy) * 8 + m8(z + dz), m4(x + dx) * 2 + (1 - c if other else c))

    yp, ym = dev(dy=1), dev(dy=-1)
    zp, zm = dev(dz=1), dev(dz=-1)
    xp, xm = dev(dx=1), dev(dx=-1)
    sib = dev(other=True)
    perm_to = (x * 8 + lax.rem(2 * lax.rem(z, 4) + c + 4, 8), lax.div(seq, 4))
    q = lax.rem(z + 4, 8)
    perm_from = (x * 8 + 4 * c + lax.div(q, 2), 2 * y + lax.rem(q, 2))

    used = [0, 0]
    sends = []

    def remote(src, dst, to, land=None):
        i = used[0]
        used[0] += 1
        copy = pltpu.make_async_remote_copy(
            src_ref=src,
            dst_ref=dst,
            send_sem=ssem.at[i],
            recv_sem=rsem.at[i],
            device_id=to,
            device_id_type=MESH,
        )
        copy.start()
        sends.append(copy)
        if land is None:
            return copy
        return pltpu.make_async_remote_copy(
            src_ref=land,
            dst_ref=land,
            send_sem=ssem.at[i],
            recv_sem=rsem.at[i],
            device_id=to,
            device_id_type=MESH,
        )

    def local(src, dst):
        i = used[1]
        used[1] += 1
        copy = pltpu.make_async_copy(src, dst, lsem.at[i])
        copy.start()
        return copy

    barrier = pltpu.get_barrier_semaphore()
    partners = [yp, ym, zp, zm, perm_to, perm_from, sib]
    partners += [dev(dx=d, other=o) for d in (1, 2, 3) for o in (False, True)]
    for partner in partners:
        pl.semaphore_signal(barrier, inc=1, device_id=partner, device_id_type=MESH)

    got_patch = [local(patch.at[:, pl.ds(o, w)], pv[i]) for i, (o, w) in enumerate(CHUNKS)]
    got_kw = local(kw, kvown.at[:, pl.ds(0, 128)])
    got_vw = local(vw, kvown.at[:, pl.ds(128, 128)])
    got_mem = local(mem, mv)
    got_w = local(wout, wv)

    idsb[0, 0] = ids[...]

    def activate(i):
        got_patch[i].wait()

        def body(r, carry):
            part = pl.ds(pl.multiple_of(r * 64, 64), 64)
            h[i][0, part, :] = gelu(pv[i][part, :].astype(F32)).astype(BF16)
            return carry

        lax.fori_loop(0, 8, body, 0)

    activate(0)
    got_kw.wait()
    got_vw.wait()
    pl.semaphore_wait(barrier, len(partners))

    yc = [{} for _ in CHUNKS]

    def y_first(i):
        yc[i]["p"] = remote(h[i].at[0], h[i].at[1], yp)
        yc[i]["m"] = remote(h[i].at[0], h[i].at[2], ym)

    def y_fwd(i, back):
        if not back:
            yc[i]["p"].wait_recv()
            part = pl.ds(0, 256)
            yc[i]["fp"] = remote(h[i].at[1, part], h[i].at[3, part], yp)
        else:
            yc[i]["m"].wait_recv()
            part = pl.ds(256, 256)
            yc[i]["fm"] = remote(h[i].at[2, part], h[i].at[3, part], ym)

    wc = {}
    rows_a, rows_b = pl.ds(0, 256 - ROWS_B), pl.ds(256 - ROWS_B, ROWS_B)
    half_a = [pl.ds(0, 128 - ROWS_B // 2), pl.ds(128 - ROWS_B // 2, 128 - ROWS_B // 2)]
    half_b = [pl.ds(256 - ROWS_B, ROWS_B // 2), pl.ds(256 - ROWS_B // 2, ROWS_B // 2)]
    perm_to_z = lax.rem(2 * lax.rem(z, 4) + c + 4, 8)

    def same(where, land, to):
        return remote(wkv.at[where], wkv.at[where], to, land=wkv.at[land])

    def once(key):
        copy = wc.pop(key, None)
        if copy is not None:
            copy.wait_recv()

    def w_perm():
        wc["perm"] = remote(kvown, wkv.at[x, perm_to_z], perm_to, land=wkv.at[y, z])

    def w_z(t, back):
        once("perm")
        once(("z", t - 1, back))
        sign, to = (-1, zm) if back else (1, zp)
        src, land = m8(z - sign * (t - 1)), m8(z - sign * t)
        part = rows_a if t <= 3 else half_a[back]
        wc["z", t, back] = same((y, src, part), (y, land, part), to)

    def w_y(t, back):
        sign, to = (-1, ym) if back else (1, yp)
        if t == 1:
            once(("z", 4, 0))
            once(("z", 4, 1))
            every = pl.ds(0, 8)
            wc["y", 1, back] = same((y, every, rows_a), (m4(y - sign), every, rows_a), to)
        else:
            once(("y", 1, back))
            some = pl.ds(4 * back, 4)
            wc["y", 2, back] = same(
                (m4(y - sign), some, rows_a), (m4(y - 2 * sign), some, rows_a), to
            )

    def b_y(t, back):
        sign, to = (-1, ym) if back else (1, yp)
        once("perm")
        once(("b", t - 1, back))
        part = rows_b if t == 1 else half_b[back]
        src, land = m4(y - sign * (t - 1)), m4(y - sign * t)
        wc["b", t, back] = same((src, z, part), (land, z, part), to)

    def b_z(t, back):
        sign, to = (-1, zm) if back else (1, zp)
        if t == 1:
            once(("b", 2, 0))
            once(("b", 2, 1))
        once(("c", t - 1, back))
        some = pl.ds(0, 4) if t <= 3 else pl.ds(2 * back, 2)
        src, land = m8(z - sign * (t - 1)), m8(z - sign * t)
        wc["c", t, back] = same((some, src, rows_b), (some, land, rows_b), to)

    ic = {}

    def i_first():
        ic["p"] = remote(idsb.at[0, 0], idsb.at[0, 1], yp)
        ic["m"] = remote(idsb.at[0, 0], idsb.at[0, 2], ym)

    def i_fwd():
        ic["p"].wait_recv()
        ic["f"] = remote(idsb.at[0, 1], idsb.at[0, 3], yp)

    def i_plane():
        for key in ("m", "f"):
            copy = ic.pop(key, None)
            if copy is not None:
                copy.wait_recv()

    def i_z(t):
        if t == 1:
            i_plane()
            ic["zp", 1] = remote(idsb.at[0], idsb.at[1], zp)
            ic["zm", 1] = remote(idsb.at[0], idsb.at[5], zm)
        else:
            ic["zp", t - 1].wait_recv()
            ic["zp", t] = remote(idsb.at[t - 1], idsb.at[t], zp)
            if t <= 3:
                ic["zm", t - 1].wait_recv()
                ic["zm", t] = remote(idsb.at[3 + t], idsb.at[4 + t], zm)

    def onehot(second):
        i_plane()

        def body(k, carry):
            step = lax.div(k + 1, 2)
            zrel = 4 + step * (1 - 2 * lax.rem(k, 2))
            base = (y * 8 + m8(z + zrel)) * 256
            slot = lax.broadcasted_iota(jnp.int32, (256, 128), 0)
            for s in range(4):
                block = idsb[0, s]
                for r in range(4):
                    row = block[r : r + 1, :] - base
                    hit = jnp.where(slot == row, 1.0, 0.0).astype(BF16)
                    oh[k, :, s * 512 + r * 128 : s * 512 + (r + 1) * 128] = hit
            return carry

        lax.fori_loop(1 if second else 0, 8 if second else 1, body, 0)

    def sums(i, k, m):
        w = CHUNKS[i][1]
        left = oh[k : k + m].reshape(m * 256, 2048)
        return jnp.dot(left, h[i][...].reshape(2048, w), preferred_element_type=F32)

    rc = [{} for _ in CHUNKS]
    lo, hi = pl.ds(0, 128), pl.ds(128, 128)

    def rs(i, t):
        if t == 0:
            yc[i]["fp"].wait_recv()
            yc[i]["fm"].wait_recv()
            p = sums(i, 0, 1).astype(BF16)
            sp[i][0, lo] = p[:128]
            sm[i][0, hi] = p[128:]
            rc[i]["p", 0] = remote(sp[i].at[0, lo], rp[i].at[0, lo], zp)
            rc[i]["m", 0] = remote(sm[i].at[0, hi], rm[i].at[0, hi], zm)
            return
        p = sums(i, 2 * t - 1, 2)
        rc[i]["p", t - 1].wait_recv()
        if t == 1:
            sp[i][t, lo] = (p[:128] + rp[i][0, lo].astype(F32)).astype(BF16)
            sp[i][t, hi] = p[128:256].astype(BF16)
        else:
            sp[i][t] = (p[:256] + rp[i][t - 1].astype(F32)).astype(BF16)
        rc[i]["p", t] = remote(sp[i].at[t], rp[i].at[t], zp)
        rc[i]["m", t - 1].wait_recv()
        if t == 1:
            sm[i][t, lo] = p[256:384].astype(BF16)
            sm[i][t, hi] = (p[384:] + rm[i][0, hi].astype(F32)).astype(BF16)
        else:
            sm[i][t] = (p[256:] + rm[i][t - 1].astype(F32)).astype(BF16)
        rc[i]["m", t] = remote(sm[i].at[t], rm[i].at[t], zm)

    xc = [{} for _ in CHUNKS]

    def rs_end(i):
        p = sums(i, 7, 1)
        rc[i]["p", 3].wait_recv()
        rc[i]["m", 3].wait_recv()
        hs[i][0] = (p + rp[i][3].astype(F32) + rm[i][3].astype(F32)).astype(BF16)
        xc[i][2] = remote(hs[i].at[0], hs[i].at[2], xp)
        xc[i][4] = remote(hs[i].at[0], hs[i].at[4], xm)
        xc[i][1] = remote(hs[i].at[0], hs[i].at[1], sib)

    def x_fwd(i, back):
        if not back:
            xc[i][2].wait_recv()
            xc[i]["fp"] = remote(hs[i].at[2, lo], hs[i].at[6, lo], xp)
            xc[i][3] = remote(hs[i].at[2], hs[i].at[3], sib)
        else:
            xc[i][4].wait_recv()
            xc[i]["fm"] = remote(hs[i].at[4, hi], hs[i].at[6, hi], xm)
            xc[i][5] = remote(hs[i].at[4], hs[i].at[5], sib)

    def x_last(i):
        xc[i]["fp"].wait_recv()
        xc[i]["fm"].wait_recv()
        xc[i][7] = remote(hs[i].at[6], hs[i].at[7], sib)

    def mm(group, pair):
        chunks = GROUPS[group]
        for i in chunks:
            xc[i][2 * pair + 1].wait_recv()
        off, w = CHUNKS[chunks[0]][0], sum(CHUNKS[i][1] for i in chunks)
        if not state.get("acc"):
            got_w.wait()
        got = None
        for b in (2 * pair, 2 * pair + 1):
            src = m4(x + (0, -1, 1, 2)[pair]) * 2 + (1 - c if b % 2 else c)
            left = jnp.concatenate([hs[i][b] for i in chunks], axis=1)
            part = jnp.dot(left, wv[src, off : off + w, :], preferred_element_type=F32)
            got = part if got is None else got + part
        if state.get("acc"):
            acc[...] = acc[...] + got
        else:
            acc[...] = got
            state["acc"] = True

    state = {}

    def count():
        ic["zp", 4].wait_recv()
        ic["zm", 3].wait_recv()
        own = seq * 256

        def body(p, carry):
            slot = lax.broadcasted_iota(jnp.int32, (256, 128), 0) + own
            for s in range(4):
                block = idsb[p, s]
                for r in range(4):
                    carry = carry + jnp.where(slot == block[r : r + 1, :], 1.0, 0.0)
            return carry

        hits = lax.fori_loop(0, 8, body, jnp.zeros((256, 128), F32))
        state["arrivals"] = jnp.broadcast_to(jnp.sum(hits, axis=1, keepdims=True), (256, 128))
        weight = jnp.transpose(jnp.broadcast_to(counts[...].astype(F32), (128, 256)))
        state["weight"] = weight
        state["share"] = 1.0 / (weight + state["arrivals"])

    table = {
        "act": activate,
        "y_first": y_first,
        "y_fwd": y_fwd,
        "w_perm": w_perm,
        "w_z": w_z,
        "w_y": w_y,
        "b_y": b_y,
        "b_z": b_z,
        "i_first": i_first,
        "i_fwd": i_fwd,
        "i_z": i_z,
        "oh": onehot,
        "rs": rs,
        "rs_end": rs_end,
        "x_fwd": x_fwd,
        "x_last": x_last,
        "mm": mm,
        "count": count,
    }
    for event, *where in ORDER:
        table[event](*where)
    arrivals, weight, share = state["arrivals"], state["weight"], state["share"]

    got_mem.wait()
    squares = jnp.zeros((256, 128), F32)
    for j in range(8):
        col = slice(j * 128, (j + 1) * 128)
        b = bias[j : j + 1, :].astype(F32)
        total = acc[:, col] + arrivals * b
        new = ((weight * mv[:, col].astype(F32) + total) * share).astype(BF16)
        mnew[:, col] = new
        stored = new.astype(F32)
        squares = squares + stored * stored
        gbuf[:, col] = (stored * gain[j : j + 1, :].astype(F32)).astype(BF16)
    put_mem = local(mnew, mem_out)
    sqc = []

    def share_squares():
        mine = jnp.broadcast_to(jnp.sum(squares, axis=1, keepdims=True), (256, 128))
        sq[0] = jnp.transpose(mine)[:8, :]
        for d in (0, 1, 2, 3):
            for o in (False, True):
                if d or o:
                    slot = 2 * d + o
                    sqc.append(remote(sq.at[0], sq.at[slot], dev(dx=d, other=o)))

    for key in list(wc):
        once(key)

    def heads(d, o):
        ys = m4(x + d)
        core = 1 - c if o else c
        total = None
        for r in range(4):
            zs = lax.rem(2 * r + core + 4, 8)
            part = jnp.dot(
                gbuf[:, r * 256 : (r + 1) * 256], wkv[ys, zs], preferred_element_type=F32
            )
            total = part if total is None else total + part
        return total

    kc = {}

    def give(d):
        ks[d] = heads(d, True).astype(BF16)
        kc[d] = remote(ks.at[d], kr.at[d], sib)

    give(2)
    p = heads(2, False)
    give(1)
    kc[2].wait_recv()
    k1s[...] = (p + kr[2].astype(F32)).astype(BF16)
    kc["p1"] = remote(k1s.at[lo], k1r.at[lo], xp)
    kc["m1"] = remote(k1s.at[hi], k1r.at[hi], xm)
    give(3)
    share_squares()
    give(0)
    for d, half, key, to in ((1, 0, "p", xp), (3, 1, "m", xm)):
        p = heads(d, False)
        kc[d].wait_recv()
        p = p + kr[d].astype(F32)
        kc[key + "1"].wait_recv()
        if half == 0:
            k2s[half, lo] = (p[:128] + k1r[lo].astype(F32)).astype(BF16)
            k2s[half, hi] = p[128:].astype(BF16)
        else:
            k2s[half, lo] = p[:128].astype(BF16)
            k2s[half, hi] = (p[128:] + k1r[hi].astype(F32)).astype(BF16)
        kc[key + "2"] = remote(k2s.at[half], k2r.at[half], to)
    p = heads(0, False)
    kc[0].wait_recv()
    p = p + kr[0].astype(F32)
    for copy in sqc:
        copy.wait_recv()
    whole = sq[0]
    for j in range(1, 8):
        whole = whole + sq[j]
    inverse = lax.rsqrt(whole[:1, :] * (1.0 / D) + 1e-06)
    inverse = jnp.transpose(jnp.broadcast_to(inverse, (128, 256)))
    kc["p2"].wait_recv()
    kc["m2"].wait_recv()
    p = p + k2r[0].astype(F32) + k2r[1].astype(F32)
    kout[...] = (p[:, :128] * inverse + kb[...].astype(F32)).astype(BF16)
    vout[...] = (p[:, 128:] * inverse + vb[...].astype(F32)).astype(BF16)
    put_key = local(kout, key_out)
    put_val = local(vout, val_out)
    for copy in sends:
        copy.wait_send()
    put_mem.wait()
    put_key.wait()
    put_val.wait()


def hand_over(a, b, c, x, y, z, sem):
    copies = [
        pltpu.make_async_copy(s, d, sem.at[i]) for i, (s, d) in enumerate(((a, x), (b, y), (c, z)))
    ]
    for copy in copies:
        copy.start()
    for copy in copies:
        copy.wait()


def on_device(patch, wout, bias, ids, mem, counts, gain, kw, vw, kb, vb):
    any_, vmem = pl.BlockSpec(memory_space=pl.ANY), pl.BlockSpec(memory_space=pltpu.VMEM)

    def per_chunk(*shape):
        return [pltpu.VMEM((*shape, w), BF16) for _, w in CHUNKS]

    scratch = [
        *per_chunk(512),
        *per_chunk(4, 512),
        pltpu.VMEM((8, 4, 4, 128), jnp.int32),
        pltpu.VMEM((8, 256, 2048), BF16),
        *per_chunk(4, 256),
        *per_chunk(4, 256),
        *per_chunk(4, 256),
        *per_chunk(4, 256),
        *per_chunk(8, 256),
        pltpu.VMEM((8, 640, 1024), BF16),
        pltpu.VMEM((256, 1024), BF16),
        pltpu.VMEM((256, 1024), F32),
        pltpu.VMEM((256, 256), BF16),
        pltpu.VMEM((4, 8, 256, 256), BF16),
        pltpu.VMEM((256, 1024), BF16),
        pltpu.VMEM((256, 1024), BF16),
        pltpu.VMEM((4, 256, 256), BF16),
        pltpu.VMEM((4, 256, 256), BF16),
        pltpu.VMEM((256, 256), BF16),
        pltpu.VMEM((256, 256), BF16),
        pltpu.VMEM((2, 256, 256), BF16),
        pltpu.VMEM((2, 256, 256), BF16),
        pltpu.VMEM((8, 8, 256), F32),
        pltpu.VMEM((256, 128), BF16),
        pltpu.VMEM((256, 128), BF16),
        pltpu.SemaphoreType.DMA((N_REMOTE,)),
        pltpu.SemaphoreType.DMA((N_REMOTE,)),
        pltpu.SemaphoreType.DMA((N_LOCAL,)),
    ]
    made = pl.pallas_call(
        kernel,
        out_shape=(
            jax.ShapeDtypeStruct((256, 1024), BF16),
            jax.ShapeDtypeStruct((256, 128), BF16),
            jax.ShapeDtypeStruct((256, 128), BF16),
        ),
        in_specs=[any_, any_, vmem, vmem, any_, vmem, vmem, any_, any_, vmem, vmem],
        out_specs=(any_, any_, any_),
        scratch_shapes=scratch,
        compiler_params=pltpu.CompilerParams(
            collective_id=0, has_side_effects=True, vmem_limit_bytes=58 * 2**20
        ),
        cost_estimate=pl.CostEstimate(
            flops=10_000_000_000, bytes_accessed=20_000_000, transcendentals=330_000
        ),
    )(
        patch,
        wout.reshape(8, 640, 1024),
        bias.reshape(8, 128),
        ids.reshape(4, 128),
        mem,
        counts.reshape(1, 256),
        gain.reshape(8, 128),
        kw,
        vw,
        kb.reshape(1, 128),
        vb.reshape(1, 128),
    )
    return pl.pallas_call(
        hand_over,
        out_shape=tuple(jax.ShapeDtypeStruct(m.shape, m.dtype) for m in made),
        in_specs=[any_, any_, any_],
        out_specs=(vmem, vmem, vmem),
        scratch_shapes=[pltpu.SemaphoreType.DMA((3,))],
    )(*made)


def solution(mesh):
    return jax.shard_map(
        on_device,
        mesh=mesh,
        in_specs=(
            P("seq", "mp"),
            P(None, "mp"),
            P("mp"),
            P("seq"),
            P("seq", "mp"),
            P("seq"),
            P("mp"),
            P("seq", "mp"),
            P("seq", "mp"),
            P("mp"),
            P("mp"),
        ),
        out_specs=(P("seq", "mp"), P("seq", "mp"), P("seq", "mp")),
        check_vma=False,
    )
```

```python
import jax
import jax.numpy as jnp
from jax import lax
from jax.experimental import pallas as pl
from jax.experimental.pallas import tpu as pltpu
from jax.sharding import PartitionSpec as P

D = 8192
CHUNKS = ((0, 128), (128, 128), (256, 128), (384, 128), (512, 128))
GROUPS = ((0, 1), (2, 3), (4,))
ROWS_B = 32
MESH = pl.DeviceIdType.MESH
N_REMOTE = 160
N_LOCAL = 12
F32, BF16 = jnp.float32, jnp.bfloat16

ORDER = (
    ("w_perm",),
    ("y_first", 0),
    ("act", 2),
    ("i_first",),
    ("act", 1),
    ("y_first", 1),
    ("w_z", 1, 0),
    ("w_z", 1, 1),
    ("i_fwd",),
    ("y_first", 2),
    ("act", 4),
    ("w_z", 2, 0),
    ("y_fwd", 1, 1),
    ("y_fwd", 1, 0),
    ("w_z", 2, 1),
    ("y_fwd", 0, 0),
    ("oh", 0),
    ("act", 3),
    ("y_fwd", 0, 1),
    ("y_first", 3),
    ("oh", 1),
    ("rs", 1, 0),
    ("b_y", 1, 1),
    ("w_z", 3, 0),
    ("w_z", 3, 1),
    ("rs", 0, 0),
    ("y_first", 4),
    ("rs", 1, 1),
    ("b_y", 1, 0),
    ("y_fwd", 3, 0),
    ("b_y", 2, 1),
    ("y_fwd", 2, 0),
    ("i_z", 1),
    ("y_fwd", 3, 1),
    ("w_z", 4, 0),
    ("w_z", 4, 1),
    ("y_fwd", 2, 1),
    ("rs", 0, 1),
    ("y_fwd", 4, 0),
    ("y_fwd", 4, 1),
    ("rs", 1, 2),
    ("b_y", 2, 0),
    ("i_z", 2),
    ("rs", 3, 0),
    ("w_y", 1, 0),
    ("w_y", 1, 1),
    ("rs", 2, 0),
    ("rs", 0, 2),
    ("rs", 4, 0),
    ("rs", 1, 3),
    ("rs", 3, 1),
    ("i_z", 3),
    ("rs", 4, 1),
    ("rs", 0, 3),
    ("rs_end", 1),
    ("rs", 2, 1),
    ("rs", 4, 2),
    ("rs", 3, 2),
    ("x_fwd", 1, 0),
    ("i_z", 4),
    ("rs_end", 0),
    ("rs", 2, 2),
    ("rs", 4, 3),
    ("b_z", 1, 1),
    ("b_z", 1, 0),
    ("rs", 3, 3),
    ("rs", 2, 3),
    ("rs_end", 4),
    ("mm", 0, 0),
    ("b_z", 2, 0),
    ("x_fwd", 0, 0),
    ("x_fwd", 0, 1),
    ("w_y", 2, 0),
    ("w_y", 2, 1),
    ("x_fwd", 1, 1),
    ("b_z", 2, 1),
    ("rs_end", 3),
    ("mm", 2, 0),
    ("rs_end", 2),
    ("x_fwd", 4, 1),
    ("x_last", 0),
    ("x_fwd", 4, 0),
    ("b_z", 3, 0),
    ("b_z", 3, 1),
    ("mm", 2, 2),
    ("x_fwd", 3, 1),
    ("x_fwd", 3, 0),
    ("count",),
    ("x_last", 1),
    ("x_fwd", 2, 0),
    ("mm", 2, 1),
    ("x_fwd", 2, 1),
    ("x_last", 4),
    ("mm", 0, 2),
    ("mm", 1, 2),
    ("mm", 2, 3),
    ("mm", 1, 1),
    ("b_z", 4, 0),
    ("b_z", 4, 1),
    ("mm", 0, 1),
    ("mm", 1, 0),
    ("x_last", 3),
    ("mm", 0, 3),
    ("x_last", 2),
    ("mm", 1, 3),
)


def gelu(v):
    return v * (1.0 + lax.erf(v * 0.7071067811865476)) * 0.5


def kernel(*refs):
    n = len(CHUNKS)
    it = iter(refs)

    def take(k):
        return [next(it) for _ in range(k)]

    patch, wout, bias, ids, mem, counts, gain, kw, vw, kb, vb = take(11)
    mem_out, key_out, val_out = take(3)
    pv, h = take(n), take(n)
    idsb, oh = take(2)
    sp, sm, rp, rm, hs = (take(n) for _ in range(5))
    wv, mv, acc, kvown, wkv, gbuf, mnew, ks, kr = take(9)
    k1s, k1r, k2s, k2r, sq, kout, vout, ssem, rsem, lsem = take(10)
    seq, mp = lax.axis_index("seq"), lax.axis_index("mp")
    y, z = lax.div(seq, 8), lax.rem(seq, 8)
    x, c = lax.div(mp, 2), lax.rem(mp, 2)

    def m4(v):
        return lax.rem(v + 4, 4)

    def m8(v):
        return lax.rem(v + 8, 8)

    def dev(dy=0, dz=0, dx=0, other=False):
        return (m4(y + dy) * 8 + m8(z + dz), m4(x + dx) * 2 + (1 - c if other else c))

    yp, ym = dev(dy=1), dev(dy=-1)
    zp, zm = dev(dz=1), dev(dz=-1)
    xp, xm = dev(dx=1), dev(dx=-1)
    sib = dev(other=True)
    perm_to = (x * 8 + lax.rem(2 * lax.rem(z, 4) + c + 4, 8), lax.div(seq, 4))
    q = lax.rem(z + 4, 8)
    perm_from = (x * 8 + 4 * c + lax.div(q, 2), 2 * y + lax.rem(q, 2))

    used = [0, 0]
    sends = []

    def remote(src, dst, to, land=None):
        i = used[0]
        used[0] += 1
        copy = pltpu.make_async_remote_copy(
            src_ref=src,
            dst_ref=dst,
            send_sem=ssem.at[i],
            recv_sem=rsem.at[i],
            device_id=to,
            device_id_type=MESH,
        )
        copy.start()
        sends.append(copy)
        if land is None:
            return copy
        return pltpu.make_async_remote_copy(
            src_ref=land,
            dst_ref=land,
            send_sem=ssem.at[i],
            recv_sem=rsem.at[i],
            device_id=to,
            device_id_type=MESH,
        )

    def local(src, dst):
        i = used[1]
        used[1] += 1
        copy = pltpu.make_async_copy(src, dst, lsem.at[i])
        copy.start()
        return copy

    barrier = pltpu.get_barrier_semaphore()
    partners = [perm_to, perm_from, yp, ym, zp, zm, sib]
    partners += [dev(dx=d, other=o) for d in (1, 2, 3) for o in (False, True)]
    for partner in partners:
        pl.semaphore_signal(barrier, inc=1, device_id=partner, device_id_type=MESH)

    got_patch = [local(patch.at[:, pl.ds(o, w)], pv[i]) for i, (o, w) in enumerate(CHUNKS)]
    got_kw = local(kw, kvown.at[:, pl.ds(0, 128)])
    got_vw = local(vw, kvown.at[:, pl.ds(128, 128)])

    idsb[0, 0] = ids[...]

    def activate(i):
        got_patch[i].wait()

        def body(r, carry):
            part = pl.ds(pl.multiple_of(r * 64, 64), 64)
            h[i][0, part, :] = gelu(pv[i][part, :].astype(F32)).astype(BF16)
            return carry

        lax.fori_loop(0, 8, body, 0)

    activate(0)
    got_kw.wait()
    got_vw.wait()
    pl.semaphore_wait(barrier, len(partners))
    got_w = local(wout, wv)
    got_mem = local(mem, mv)

    yc = [{} for _ in CHUNKS]

    def y_first(i):
        yc[i]["p"] = remote(h[i].at[0], h[i].at[1], yp)
        yc[i]["m"] = remote(h[i].at[0], h[i].at[2], ym)

    def y_fwd(i, back):
        if not back:
            yc[i]["p"].wait_recv()
            part = pl.ds(0, 256)
            yc[i]["fp"] = remote(h[i].at[1, part], h[i].at[3, part], yp)
        else:
            yc[i]["m"].wait_recv()
            part = pl.ds(256, 256)
            yc[i]["fm"] = remote(h[i].at[2, part], h[i].at[3, part], ym)

    wc = {}
    rows_a, rows_b = pl.ds(0, 256 - ROWS_B), pl.ds(256 - ROWS_B, ROWS_B)
    half_a = [pl.ds(0, 128 - ROWS_B // 2), pl.ds(128 - ROWS_B // 2, 128 - ROWS_B // 2)]
    half_b = [pl.ds(256 - ROWS_B, ROWS_B // 2), pl.ds(256 - ROWS_B // 2, ROWS_B // 2)]
    perm_to_z = lax.rem(2 * lax.rem(z, 4) + c + 4, 8)

    def same(where, land, to):
        return remote(wkv.at[where], wkv.at[where], to, land=wkv.at[land])

    def once(key):
        copy = wc.pop(key, None)
        if copy is not None:
            copy.wait_recv()

    def w_perm():
        wc["perm"] = remote(kvown, wkv.at[x, perm_to_z], perm_to, land=wkv.at[y, z])

    def w_z(t, back):
        once("perm")
        once(("z", t - 1, back))
        sign, to = (-1, zm) if back else (1, zp)
        src, land = m8(z - sign * (t - 1)), m8(z - sign * t)
        part = rows_a if t <= 3 else half_a[back]
        wc["z", t, back] = same((y, src, part), (y, land, part), to)

    def w_y(t, back):
        sign, to = (-1, ym) if back else (1, yp)
        if t == 1:
            once(("z", 4, 0))
            once(("z", 4, 1))
            every = pl.ds(0, 8)
            wc["y", 1, back] = same((y, every, rows_a), (m4(y - sign), every, rows_a), to)
        else:
            once(("y", 1, back))
            some = pl.ds(4 * back, 4)
            wc["y", 2, back] = same(
                (m4(y - sign), some, rows_a), (m4(y - 2 * sign), some, rows_a), to
            )

    def b_y(t, back):
        sign, to = (-1, ym) if back else (1, yp)
        once("perm")
        once(("b", t - 1, back))
        part = rows_b if t == 1 else half_b[back]
        src, land = m4(y - sign * (t - 1)), m4(y - sign * t)
        wc["b", t, back] = same((src, z, part), (land, z, part), to)

    def b_z(t, back):
        sign, to = (-1, zm) if back else (1, zp)
        if t == 1:
            once(("b", 2, 0))
            once(("b", 2, 1))
        once(("c", t - 1, back))
        some = pl.ds(0, 4) if t <= 3 else pl.ds(2 * back, 2)
        src, land = m8(z - sign * (t - 1)), m8(z - sign * t)
        wc["c", t, back] = same((some, src, rows_b), (some, land, rows_b), to)

    ic = {}

    def i_first():
        ic["p"] = remote(idsb.at[0, 0], idsb.at[0, 1], yp)
        ic["m"] = remote(idsb.at[0, 0], idsb.at[0, 2], ym)

    def i_fwd():
        ic["p"].wait_recv()
        ic["f"] = remote(idsb.at[0, 1], idsb.at[0, 3], yp)

    def i_plane():
        for key in ("m", "f"):
            copy = ic.pop(key, None)
            if copy is not None:
                copy.wait_recv()

    def i_z(t):
        if t == 1:
            i_plane()
            ic["zp", 1] = remote(idsb.at[0], idsb.at[1], zp)
            ic["zm", 1] = remote(idsb.at[0], idsb.at[5], zm)
        else:
            ic["zp", t - 1].wait_recv()
            ic["zp", t] = remote(idsb.at[t - 1], idsb.at[t], zp)
            if t <= 3:
                ic["zm", t - 1].wait_recv()
                ic["zm", t] = remote(idsb.at[3 + t], idsb.at[4 + t], zm)

    def onehot(second):
        i_plane()

        def body(k, carry):
            step = lax.div(k + 1, 2)
            zrel = 4 + step * (1 - 2 * lax.rem(k, 2))
            base = (y * 8 + m8(z + zrel)) * 256
            slot = lax.broadcasted_iota(jnp.int32, (256, 128), 0)
            for s in range(4):
                block = idsb[0, s]
                for r in range(4):
                    row = block[r : r + 1, :] - base
                    hit = jnp.where(slot == row, 1.0, 0.0).astype(BF16)
                    oh[k, :, s * 512 + r * 128 : s * 512 + (r + 1) * 128] = hit
            return carry

        lax.fori_loop(1 if second else 0, 8 if second else 1, body, 0)

    def sums(i, k, m):
        w = CHUNKS[i][1]
        left = oh[k : k + m].reshape(m * 256, 2048)
        return jnp.dot(left, h[i][...].reshape(2048, w), preferred_element_type=F32)

    rc = [{} for _ in CHUNKS]
    lo, hi = pl.ds(0, 128), pl.ds(128, 128)

    def rs(i, t):
        if t == 0:
            yc[i]["fp"].wait_recv()
            yc[i]["fm"].wait_recv()
            p = sums(i, 0, 1).astype(BF16)
            sp[i][0, lo] = p[:128]
            sm[i][0, hi] = p[128:]
            rc[i]["p", 0] = remote(sp[i].at[0, lo], rp[i].at[0, lo], zp)
            rc[i]["m", 0] = remote(sm[i].at[0, hi], rm[i].at[0, hi], zm)
            return
        p = sums(i, 2 * t - 1, 2)
        rc[i]["p", t - 1].wait_recv()
        if t == 1:
            sp[i][t, lo] = (p[:128] + rp[i][0, lo].astype(F32)).astype(BF16)
            sp[i][t, hi] = p[128:256].astype(BF16)
        else:
            sp[i][t] = (p[:256] + rp[i][t - 1].astype(F32)).astype(BF16)
        rc[i]["p", t] = remote(sp[i].at[t], rp[i].at[t], zp)
        rc[i]["m", t - 1].wait_recv()
        if t == 1:
            sm[i][t, lo] = p[256:384].astype(BF16)
            sm[i][t, hi] = (p[384:] + rm[i][0, hi].astype(F32)).astype(BF16)
        else:
            sm[i][t] = (p[256:] + rm[i][t - 1].astype(F32)).astype(BF16)
        rc[i]["m", t] = remote(sm[i].at[t], rm[i].at[t], zm)

    xc = [{} for _ in CHUNKS]

    def rs_end(i):
        p = sums(i, 7, 1)
        rc[i]["p", 3].wait_recv()
        rc[i]["m", 3].wait_recv()
        hs[i][0] = (p + rp[i][3].astype(F32) + rm[i][3].astype(F32)).astype(BF16)
        xc[i][2] = remote(hs[i].at[0], hs[i].at[2], xp)
        xc[i][4] = remote(hs[i].at[0], hs[i].at[4], xm)
        xc[i][1] = remote(hs[i].at[0], hs[i].at[1], sib)

    def x_fwd(i, back):
        if not back:
            xc[i][2].wait_recv()
            xc[i]["fp"] = remote(hs[i].at[2, lo], hs[i].at[6, lo], xp)
            xc[i][3] = remote(hs[i].at[2], hs[i].at[3], sib)
        else:
            xc[i][4].wait_recv()
            xc[i]["fm"] = remote(hs[i].at[4, hi], hs[i].at[6, hi], xm)
            xc[i][5] = remote(hs[i].at[4], hs[i].at[5], sib)

    def x_last(i):
        xc[i]["fp"].wait_recv()
        xc[i]["fm"].wait_recv()
        xc[i][7] = remote(hs[i].at[6], hs[i].at[7], sib)

    def mm(group, pair):
        chunks = GROUPS[group]
        for i in chunks:
            xc[i][2 * pair + 1].wait_recv()
        off, w = CHUNKS[chunks[0]][0], sum(CHUNKS[i][1] for i in chunks)
        if not state.get("acc"):
            got_w.wait()
        got = None
        for b in (2 * pair, 2 * pair + 1):
            src = m4(x + (0, -1, 1, 2)[pair]) * 2 + (1 - c if b % 2 else c)
            left = jnp.concatenate([hs[i][b] for i in chunks], axis=1)
            part = jnp.dot(left, wv[src, off : off + w, :], preferred_element_type=F32)
            got = part if got is None else got + part
        if state.get("acc"):
            acc[...] = acc[...] + got
        else:
            acc[...] = got
            state["acc"] = True

    state = {}

    def count():
        ic["zp", 4].wait_recv()
        ic["zm", 3].wait_recv()
        own = seq * 256

        def body(p, carry):
            slot = lax.broadcasted_iota(jnp.int32, (256, 128), 0) + own
            for s in range(4):
                block = idsb[p, s]
                for r in range(4):
                    carry = carry + jnp.where(slot == block[r : r + 1, :], 1.0, 0.0)
            return carry

        hits = lax.fori_loop(0, 8, body, jnp.zeros((256, 128), F32))
        state["arrivals"] = jnp.broadcast_to(jnp.sum(hits, axis=1, keepdims=True), (256, 128))
        weight = jnp.transpose(jnp.broadcast_to(counts[...].astype(F32), (128, 256)))
        state["weight"] = weight
        state["share"] = 1.0 / (weight + state["arrivals"])

    table = {
        "act": activate,
        "y_first": y_first,
        "y_fwd": y_fwd,
        "w_perm": w_perm,
        "w_z": w_z,
        "w_y": w_y,
        "b_y": b_y,
        "b_z": b_z,
        "i_first": i_first,
        "i_fwd": i_fwd,
        "i_z": i_z,
        "oh": onehot,
        "rs": rs,
        "rs_end": rs_end,
        "x_fwd": x_fwd,
        "x_last": x_last,
        "mm": mm,
        "count": count,
    }
    for event, *where in ORDER:
        table[event](*where)
    arrivals, weight, share = state["arrivals"], state["weight"], state["share"]

    got_mem.wait()
    squares = jnp.zeros((256, 128), F32)
    for j in range(8):
        col = slice(j * 128, (j + 1) * 128)
        b = bias[j : j + 1, :].astype(F32)
        total = acc[:, col] + arrivals * b
        new = ((weight * mv[:, col].astype(F32) + total) * share).astype(BF16)
        mnew[:, col] = new
        stored = new.astype(F32)
        squares = squares + stored * stored
        gbuf[:, col] = (stored * gain[j : j + 1, :].astype(F32)).astype(BF16)
    put_mem = local(mnew, mem_out)
    sqc = []

    def share_squares():
        mine = jnp.broadcast_to(jnp.sum(squares, axis=1, keepdims=True), (256, 128))
        sq[0] = jnp.transpose(mine)[:8, :]
        for d in (0, 1, 2, 3):
            for o in (False, True):
                if d or o:
                    slot = 2 * d + o
                    sqc.append(remote(sq.at[0], sq.at[slot], dev(dx=d, other=o)))

    for key in list(wc):
        once(key)

    def heads(d, o):
        ys = m4(x + d)
        core = 1 - c if o else c
        total = None
        for r in range(4):
            zs = lax.rem(2 * r + core + 4, 8)
            part = jnp.dot(
                gbuf[:, r * 256 : (r + 1) * 256], wkv[ys, zs], preferred_element_type=F32
            )
            total = part if total is None else total + part
        return total

    kc = {}

    def give(d):
        ks[d] = heads(d, True).astype(BF16)
        kc[d] = remote(ks.at[d], kr.at[d], sib)

    give(2)
    p = heads(2, False)
    give(1)
    kc[2].wait_recv()
    k1s[...] = (p + kr[2].astype(F32)).astype(BF16)
    kc["p1"] = remote(k1s.at[lo], k1r.at[lo], xp)
    kc["m1"] = remote(k1s.at[hi], k1r.at[hi], xm)
    give(3)
    share_squares()
    give(0)
    for d, half, key, to in ((1, 0, "p", xp), (3, 1, "m", xm)):
        p = heads(d, False)
        kc[d].wait_recv()
        p = p + kr[d].astype(F32)
        kc[key + "1"].wait_recv()
        if half == 0:
            k2s[half, lo] = (p[:128] + k1r[lo].astype(F32)).astype(BF16)
            k2s[half, hi] = p[128:].astype(BF16)
        else:
            k2s[half, lo] = p[:128].astype(BF16)
            k2s[half, hi] = (p[128:] + k1r[hi].astype(F32)).astype(BF16)
        kc[key + "2"] = remote(k2s.at[half], k2r.at[half], to)
    p = heads(0, False)
    kc[0].wait_recv()
    p = p + kr[0].astype(F32)
    for copy in sqc:
        copy.wait_recv()
    whole = sq[0]
    for j in range(1, 8):
        whole = whole + sq[j]
    inverse = lax.rsqrt(whole[:1, :] * (1.0 / D) + 1e-06)
    inverse = jnp.transpose(jnp.broadcast_to(inverse, (128, 256)))
    kc["p2"].wait_recv()
    kc["m2"].wait_recv()
    p = p + k2r[0].astype(F32) + k2r[1].astype(F32)
    kout[...] = (p[:, :128] * inverse + kb[...].astype(F32)).astype(BF16)
    vout[...] = (p[:, 128:] * inverse + vb[...].astype(F32)).astype(BF16)
    put_key = local(kout, key_out)
    put_val = local(vout, val_out)
    for copy in sends:
        copy.wait_send()
    put_mem.wait()
    put_key.wait()
    put_val.wait()


def hand_over(a, b, c, x, y, z, sem):
    copies = [
        pltpu.make_async_copy(s, d, sem.at[i]) for i, (s, d) in enumerate(((a, x), (b, y), (c, z)))
    ]
    for copy in copies:
        copy.start()
    for copy in copies:
        copy.wait()


def on_device(patch, wout, bias, ids, mem, counts, gain, kw, vw, kb, vb):
    any_, vmem = pl.BlockSpec(memory_space=pl.ANY), pl.BlockSpec(memory_space=pltpu.VMEM)

    def per_chunk(*shape):
        return [pltpu.VMEM((*shape, w), BF16) for _, w in CHUNKS]

    scratch = [
        *per_chunk(512),
        *per_chunk(4, 512),
        pltpu.VMEM((8, 4, 4, 128), jnp.int32),
        pltpu.VMEM((8, 256, 2048), BF16),
        *per_chunk(4, 256),
        *per_chunk(4, 256),
        *per_chunk(4, 256),
        *per_chunk(4, 256),
        *per_chunk(8, 256),
        pltpu.VMEM((8, 640, 1024), BF16),
        pltpu.VMEM((256, 1024), BF16),
        pltpu.VMEM((256, 1024), F32),
        pltpu.VMEM((256, 256), BF16),
        pltpu.VMEM((4, 8, 256, 256), BF16),
        pltpu.VMEM((256, 1024), BF16),
        pltpu.VMEM((256, 1024), BF16),
        pltpu.VMEM((4, 256, 256), BF16),
        pltpu.VMEM((4, 256, 256), BF16),
        pltpu.VMEM((256, 256), BF16),
        pltpu.VMEM((256, 256), BF16),
        pltpu.VMEM((2, 256, 256), BF16),
        pltpu.VMEM((2, 256, 256), BF16),
        pltpu.VMEM((8, 8, 256), F32),
        pltpu.VMEM((256, 128), BF16),
        pltpu.VMEM((256, 128), BF16),
        pltpu.SemaphoreType.DMA((N_REMOTE,)),
        pltpu.SemaphoreType.DMA((N_REMOTE,)),
        pltpu.SemaphoreType.DMA((N_LOCAL,)),
    ]
    made = pl.pallas_call(
        kernel,
        out_shape=(
            jax.ShapeDtypeStruct((256, 1024), BF16),
            jax.ShapeDtypeStruct((256, 128), BF16),
            jax.ShapeDtypeStruct((256, 128), BF16),
        ),
        in_specs=[any_, any_, vmem, vmem, any_, vmem, vmem, any_, any_, vmem, vmem],
        out_specs=(any_, any_, any_),
        scratch_shapes=scratch,
        compiler_params=pltpu.CompilerParams(
            collective_id=0, has_side_effects=True, vmem_limit_bytes=58 * 2**20
        ),
        cost_estimate=pl.CostEstimate(
            flops=10_000_000_000, bytes_accessed=20_000_000, transcendentals=330_000
        ),
    )(
        patch,
        wout.reshape(8, 640, 1024),
        bias.reshape(8, 128),
        ids.reshape(4, 128),
        mem,
        counts.reshape(1, 256),
        gain.reshape(8, 128),
        kw,
        vw,
        kb.reshape(1, 128),
        vb.reshape(1, 128),
    )
    return pl.pallas_call(
        hand_over,
        out_shape=tuple(jax.ShapeDtypeStruct(m.shape, m.dtype) for m in made),
        in_specs=[any_, any_, any_],
        out_specs=(vmem, vmem, vmem),
        scratch_shapes=[pltpu.SemaphoreType.DMA((3,))],
    )(*made)


def solution(mesh):
    return jax.shard_map(
        on_device,
        mesh=mesh,
        in_specs=(
            P("seq", "mp"),
            P(None, "mp"),
            P("mp"),
            P("seq"),
            P("seq", "mp"),
            P("seq"),
            P("mp"),
            P("seq", "mp"),
            P("seq", "mp"),
            P("mp"),
            P("mp"),
        ),
        out_specs=(P("seq", "mp"), P("seq", "mp"), P("seq", "mp")),
        check_vma=False,
    )
```
